32 devices in a mesh: sens: 2 (over y), par: 16 (over z, x, core).
Axes of the slice: x: 2, y: 2, z: 4, core: 2. Of those that a mesh axis runs over, the one named last changes fastest.
Arguments:
- probes: bfloat16 [2, 256, 512], P(None, 'sens', 'par'), may hold values from -6 to 6
- green_blocks: bfloat16 [2, 16384, 256], P(None, 'par', 'sens'), may hold values from -0.375 to 0.375
- noise_table: float32 [4, 8], replicated, may hold values from 0.3 to 4
- station_class: int32 [256], P('sens'), may hold values from 0 to 7
- kappa_table: float32 [16], replicated, may hold values from 0.1 to 4
- coeff_index: int32 [4096], replicated, may hold values from 0 to 15
Outputs:
- hess_probes: float32 [2, 256, 512], P(None, 'sens', 'par')
The draws below stay inside these ranges and needn't reach their ends.
All inputs are finite; a program needn't handle non-finite values.
Results may differ from the reference program's by a relative error of at most 0.003.
Values may be sent and summed in bfloat16 or wider, within the bound.
No kernel may reach another device: no remote copies, remote signals or barrier semaphores. Data moves between devices by JAX's collectives and lax.ppermute only.
A program may use at most 64 MiB of HBM per device.

```python
import math
import jax
import jax.numpy as jnp
from jax import lax

SPLIT = 4
DIP = 32
PROBES = 128
CLASSES = 16
GROUPS = 8
NFREQ = 4
SENSORS = 256
STRIKE = 128
CELLS = 4096
ROWS = 512


def set_ends(entries, own_key, smallest, largest):
    dims = entries.shape
    index_at = [jax.random.randint(jax.random.fold_in(own_key, axis), (), 0, dims[axis]) for axis in range(len(dims))]
    entries = entries.at[tuple(index_at)].set(smallest)
    longest = dims.index(max(dims))
    index_at[longest] = (index_at[longest] + 1) % dims[longest]
    return entries.at[tuple(index_at)].set(largest)


def block_levels(key, extent, shards, least, largest):
    def one(axis_at, parts):
        draws = jax.random.uniform(jax.random.fold_in(jax.random.fold_in(key, 6), axis_at), (parts,), jnp.float32, least / len(shards), largest / len(shards))
        return jnp.repeat(jnp.exp(draws), extent[axis_at] // parts).reshape((-1,) + (1,) * (len(extent) - axis_at - 1))

    loudness = one(*shards[0])
    for cut in shards[1:]:
        loudness = loudness * one(*cut)
    return loudness


def normal_values(stream_key, dims, deviation, limit, shards=(), kind=jnp.bfloat16):
    loudness = block_levels(stream_key, dims, shards, -0.22, 0.18) if shards else 1.0
    result = jax.random.normal(stream_key, dims, jnp.float32) * deviation * loudness
    return jnp.minimum(jnp.maximum(result, -limit), limit).astype(kind)


def setup_inputs(seed: int = 0) -> dict:
    streams_of = jax.random.split(jax.random.key(seed), 7)
    return {
        "probes": normal_values(streams_of[0], (2, SENSORS, ROWS), 1.0, 6.0, ((1, 2), (2, 16))),
        "green_blocks": normal_values(streams_of[1], (2, NFREQ * CELLS, SENSORS), SENSORS ** -0.5, 0.375, ((1, 16), (2, 2))),
        "noise_table": jnp.clip(jnp.exp(jax.random.uniform(streams_of[2], (NFREQ, GROUPS), jnp.float32, math.log(0.3), math.log(4.0))), 0.3, 4.0),
        "station_class": set_ends(jax.random.randint(streams_of[3], (SENSORS,), 0, GROUPS), jax.random.fold_in(streams_of[3], 1), 0, GROUPS - 1).astype(jnp.int32),
        "kappa_table": jnp.clip(jnp.exp(jax.random.uniform(streams_of[4], (CLASSES,), jnp.float32, math.log(0.1), math.log(4.0))), 0.1, 4.0),
        "coeff_index": set_ends(jax.random.randint(streams_of[5], (CELLS,), 0, CLASSES), jax.random.fold_in(streams_of[5], 1), 0, CLASSES - 1).astype(jnp.int32),
    }


def neighbours(values):
    padded = jnp.pad(values, ((0, 0), (1, 1), (1, 1), (0, 0)))
    summed = padded[:, 2:, 1:-1] + padded[:, :-2, 1:-1]
    return summed + padded[:, 1:-1, 2:] + padded[:, 1:-1, :-2]

def reference(probes, green_blocks, noise_table, station_class, kappa_table, coeff_index):
    part_probes = PROBES // SPLIT
    part_cells = CELLS // SPLIT
    weight = 1.0 / jnp.sqrt(noise_table[:, station_class].T)
    wrow = jnp.tile(jnp.repeat(weight, part_probes, axis=1), (1, SPLIT))
    weighted = (wrow[None] * probes.astype(jnp.float32)).astype(jnp.bfloat16)
    weighted = weighted.reshape(2, SENSORS, SPLIT, NFREQ, part_probes)
    green_split = green_blocks.reshape(2, SPLIT, NFREQ, part_cells, SENSORS)
    diagonal = (4.0 + kappa_table[coeff_index]).reshape(1, STRIKE, DIP, 1)

    def one_freq(freq_pos):
        green_part = lax.dynamic_index_in_dim(green_split, freq_pos, 2, keepdims=False).reshape(2, CELLS, SENSORS)
        probe_part = lax.dynamic_index_in_dim(weighted, freq_pos, 3, keepdims=False).reshape(2, SENSORS, PROBES)
        real_src = jnp.dot(green_part[0], probe_part[0], preferred_element_type=jnp.float32) + jnp.dot(green_part[1], probe_part[1], preferred_element_type=jnp.float32)
        imag_src = jnp.dot(green_part[0], probe_part[1], preferred_element_type=jnp.float32) - jnp.dot(green_part[1], probe_part[0], preferred_element_type=jnp.float32)
        source = jnp.stack([real_src, imag_src]).reshape(2, STRIKE, DIP, PROBES)
        first_sweep = source / diagonal
        second_sweep = (source + neighbours(first_sweep)) / diagonal
        slip_tile = ((source + neighbours(second_sweep)) / diagonal).astype(jnp.bfloat16).reshape(2, CELLS, PROBES)
        real_data = jnp.dot(green_part[0].T, slip_tile[0], preferred_element_type=jnp.float32) - jnp.dot(green_part[1].T, slip_tile[1], preferred_element_type=jnp.float32)
        imag_data = jnp.dot(green_part[0].T, slip_tile[1], preferred_element_type=jnp.float32) + jnp.dot(green_part[1].T, slip_tile[0], preferred_element_type=jnp.float32)
        return jnp.stack([real_data, imag_data])
    data_sum = lax.map(one_freq, jnp.arange(NFREQ, dtype=jnp.int32))
    data_sum = data_sum.reshape(NFREQ, 2, SENSORS, SPLIT, part_probes)
    data_sum = data_sum.transpose(1, 2, 3, 0, 4).reshape(2, SENSORS, ROWS)
    return wrow[None] * data_sum
```

```python
import functools

import jax
import jax.numpy as jnp
from jax import lax
from jax.experimental import pallas as pl
from jax.experimental.pallas import tpu as pltpu
from jax.sharding import PartitionSpec as P

SPLIT = 4
DIP = 32
LANES = 128
REACH = 2 * DIP
F32 = jnp.float32
BF16 = jnp.bfloat16


def swapped(value, axis, mask):
    return lax.ppermute(value, axis, [(i, i ^ mask) for i in range(lax.axis_size(axis))])


def turned(value, axis, step):
    size = lax.axis_size(axis)
    return lax.ppermute(value, axis, [(i, (i + step) % size) for i in range(size)])


def shifted(value, axis, step):
    size = lax.axis_size(axis)
    return lax.ppermute(value, axis, [(i, i + step) for i in range(size) if 0 <= i + step < size])


def dot(a, b, form=((1,), (0,))):
    return lax.dot_general(a, b, (form, ((), ())), preferred_element_type=F32)


def chosen(table, index, count, place):
    value = jnp.zeros(index.shape, F32)
    for k in range(count):
        value = jnp.where(index == k, place(table, k), value)
    return value


def stencil():
    row = lax.broadcasted_iota(jnp.int32, (4 * LANES, 2 * LANES), 0)
    col = lax.broadcasted_iota(jnp.int32, (4 * LANES, 2 * LANES), 1)
    away = row - LANES - col
    dip = lax.rem(col, DIP)
    hit = (away == DIP) | (away == -DIP)
    hit = hit | ((away == 1) & (dip != DIP - 1)) | ((away == -1) & (dip != 0))
    return hit.astype(F32).astype(BF16)


def local_kernel(nsens, nfreq, nclass, ngroup, noise, kappa, coeff, *refs):
    stations, refs = refs[:nsens], refs[nsens:]
    probes, refs = refs[:nsens], refs[nsens:]
    greens, refs = refs[:nsens], refs[nsens:]
    low, high, keep, send = refs
    par = lax.axis_index("par")
    freq = lax.rem(par, nfreq)
    part = lax.div(par, nfreq)
    cells = greens[0].shape[1]
    blocks = cells // LANES
    rows = probes[0].shape[0] * probes[0].shape[2]
    parts = coeff.shape[0] // blocks

    def weight(station):
        variance = chosen(noise, station[...], ngroup, lambda t, k: t[freq, k])
        return 1.0 / jnp.sqrt(variance)

    def inverse(index):
        return 1.0 / (4.0 + chosen(kappa, index, nclass, lambda t, k: t[k]))

    own = inverse(coeff[pl.ds(part * blocks, blocks), :])
    before = inverse(coeff[pl.ds(jnp.maximum(part * blocks - 1, 0), 1), :])
    after = inverse(coeff[pl.ds(jnp.minimum((part + 1) * blocks, parts * blocks - 1), 1), :])
    inv = [jnp.where(part > 0, before, 0.0)]
    inv += [own[b : b + 1] for b in range(blocks)]
    inv += [jnp.where(part < parts - 1, after, 0.0)]

    weights = [weight(s) for s in stations]
    lhs = []
    for w, p in zip(weights, probes):
        z = (w[None, None] * p[...].astype(F32)).astype(BF16)
        zr, zi = z[:, 0].reshape(rows, LANES), z[:, 1].reshape(rows, LANES)
        top = jnp.concatenate([zr, zi], axis=1)
        bottom = jnp.concatenate([zi, -zr], axis=1)
        lhs.append(jnp.concatenate([top, bottom], axis=0))

    def both(ref, b, n):
        return jnp.concatenate([ref[0, b : b + n], ref[1, b : b + n]], axis=1)

    wide = 2 * LANES
    source = []
    for b in range(0, cells, wide):
        total = dot(lhs[0], both(greens[0], b, wide), ((1,), (1,)))
        for a, g in zip(lhs[1:], greens[1:]):
            total = total + dot(a, both(g, b, wide), ((1,), (1,)))
        source += [total[:, :LANES], total[:, LANES:]]
    zero = jnp.zeros((2 * rows, LANES), BF16)
    hood = stencil()

    def sums(u):
        out = []
        for c in range(0, blocks + 2, 2):
            lo, hi = max(c - 1, 0), min(c + 3, blocks + 2)
            window = jnp.concatenate(u[lo:hi], axis=1)
            total = dot(window, hood[(lo - c + 1) * LANES : (hi - c + 1) * LANES])
            out += [total[:, :LANES], total[:, LANES:]]
        return out

    def solved(n):
        out = []
        for b in range(blocks + 2):
            inner = 0 < b <= blocks
            value = source[b - 1] + n[b] if inner else n[b]
            out.append((value * inv[b]).astype(BF16))
        return out

    first = [zero] + [(source[b] * inv[b + 1]).astype(BF16) for b in range(blocks)] + [zero]
    slip = solved(sums(solved(sums(first))))
    data = dot(jnp.concatenate(slip[1:-1], axis=1), both(greens[0], 0, cells))
    pad = jnp.zeros((LANES - REACH, 2 * LANES), BF16)
    data = data + dot(slip[0], jnp.concatenate([pad, both(low, 0, REACH)], axis=0))
    data = data + dot(slip[-1], jnp.concatenate([both(high, 0, REACH), pad], axis=0))
    real = weights[0] * (data[:rows, :LANES] - data[rows:, LANES:])
    imag = weights[0] * (data[rows:, :LANES] + data[:rows, LANES:])
    half = rows // 2
    keep[0], keep[1] = real[:half], imag[:half]
    send[0], send[1] = real[half:].astype(BF16), imag[half:].astype(BF16)


def shards(probes, green_blocks, noise_table, station_class, kappa_table, coeff_index):
    nfreq, ngroup = noise_table.shape
    nsens = lax.axis_size("sens")
    rows_dev = probes.shape[2]
    vector = jnp.transpose(probes, (0, 2, 1))
    station = station_class.reshape(1, -1)

    greens = [green_blocks] + [turned(green_blocks, "sens", k) for k in range(1, nsens)]
    mine = vector[None]
    for mask in (2 * nfreq, nfreq):
        mine = jnp.concatenate([mine, swapped(mine, "par", mask)], axis=0)
    low = shifted(green_blocks[:, -REACH:], "par", nfreq)
    high = shifted(green_blocks[:, :REACH], "par", -nfreq)
    vectors = [mine] + [turned(mine, "sens", k) for k in range(1, nsens)]
    stations = [station] + [turned(station, "sens", k) for k in range(1, nsens)]

    smem = pl.BlockSpec(memory_space=pltpu.SMEM)
    vmem = pl.BlockSpec(memory_space=pltpu.VMEM)
    half = SPLIT // 2 * rows_dev
    sensors = probes.shape[1]
    kernel = functools.partial(local_kernel, nsens, nfreq, kappa_table.shape[0], ngroup)
    keep, send = pl.pallas_call(
        kernel,
        out_shape=[
            jax.ShapeDtypeStruct((2, half, sensors), F32),
            jax.ShapeDtypeStruct((2, half, sensors), BF16),
        ],
        in_specs=[smem, smem] + [vmem] * (3 + 3 * nsens),
        out_specs=[vmem, vmem],
        compiler_params=pltpu.CompilerParams(vmem_limit_bytes=32 * 2**20),
    )(
        noise_table,
        kappa_table,
        coeff_index.reshape(-1, LANES),
        *stations,
        *vectors,
        *greens,
        low,
        high,
    )
    near = keep + swapped(send, "par", nfreq).astype(F32)
    far = swapped(near[:, rows_dev:].astype(BF16), "par", 2 * nfreq)
    return jnp.transpose(near[:, :rows_dev] + far.astype(F32), (0, 2, 1))


def solution(mesh):
    in_specs = (P(None, "sens", "par"), P(None, "par", "sens"), P(), P("sens"), P(), P())
    out_specs = P(None, "sens", "par")
    return jax.shard_map(shards, mesh=mesh, in_specs=in_specs, out_specs=out_specs, check_vma=False)
```

```python
import functools

import jax
import jax.numpy as jnp
from jax import lax
from jax.experimental import pallas as pl
from jax.experimental.pallas import tpu as pltpu
from jax.sharding import PartitionSpec as P

SPLIT = 4
DIP = 32
LANES = 128
REACH = 2 * DIP
F32 = jnp.float32
BF16 = jnp.bfloat16
PARAMS = pltpu.CompilerParams(vmem_limit_bytes=32 * 2**20)


def swapped(value, axis, mask):
    return lax.ppermute(value, axis, [(i, i ^ mask) for i in range(lax.axis_size(axis))])


def turned(value, axis, step):
    size = lax.axis_size(axis)
    return lax.ppermute(value, axis, [(i, (i + step) % size) for i in range(size)])


def crossed(value, axis, nfreq):
    pairs = [(p * nfreq + f, (p + 1) * nfreq + f) for p in range(1, SPLIT - 1, 2) for f in range(nfreq)]
    return lax.ppermute(value, axis, pairs + [(b, a) for a, b in pairs])


def dot(a, b, form=((1,), (0,))):
    return lax.dot_general(a, b, (form, ((), ())), preferred_element_type=F32)


def chosen(table, index, count, place):
    value = jnp.zeros(index.shape, F32)
    for k in range(count):
        value = jnp.where(index == k, place(table, k), value)
    return value


def stencil():
    row = lax.broadcasted_iota(jnp.int32, (4 * LANES, 2 * LANES), 0)
    col = lax.broadcasted_iota(jnp.int32, (4 * LANES, 2 * LANES), 1)
    away = row - LANES - col
    dip = lax.rem(col, DIP)
    hit = (away == DIP) | (away == -DIP)
    hit = hit | ((away == 1) & (dip != DIP - 1)) | ((away == -1) & (dip != 0))
    return hit.astype(F32).astype(BF16)


def planes(ref, b, n):
    return jnp.concatenate([ref[0, b : b + n], ref[1, b : b + n]], axis=1)


def lhs(z):
    rows = z.shape[0] * z.shape[2]
    zr, zi = z[:, 0].reshape(rows, LANES), z[:, 1].reshape(rows, LANES)
    top = jnp.concatenate([zr, zi], axis=1)
    return jnp.concatenate([top, jnp.concatenate([zi, -zr], axis=1)], axis=0)


def own_kernel(nfreq, nclass, kappa, coeff, vector, green, operator, source, inverse, hood):
    part = lax.div(lax.axis_index("par"), nfreq)
    cells = green.shape[1]
    blocks = cells // LANES
    parts = coeff.shape[0] // blocks

    def inv(index):
        return 1.0 / (4.0 + chosen(kappa, index, nclass, lambda t, k: t[k]))

    before = inv(coeff[pl.ds(jnp.maximum(part * blocks - 1, 0), 1), :])
    after = inv(coeff[pl.ds(jnp.minimum((part + 1) * blocks, parts * blocks - 1), 1), :])
    inverse[0:blocks, :] = inv(coeff[pl.ds(part * blocks, blocks), :])
    inverse[blocks : blocks + 1, :] = jnp.where(part < parts - 1, after, 0.0)
    inverse[blocks + 1 : blocks + 2, :] = jnp.where(part > 0, before, 0.0)
    hood[...] = stencil()
    both = planes(green, 0, cells)
    operator[...] = both
    source[...] = dot(lhs(vector[...]), both, ((1,), (1,)))


def slip_kernel(nfreq, nsens, weight, inverse, hood, source, operator, facing, other, *refs):
    vectors, refs = refs[: nsens - 1], refs[nsens - 1 :]
    greens, (keep, send) = refs[: nsens - 1], refs[nsens - 1 :]
    part = lax.div(lax.axis_index("par"), nfreq)
    cells = operator.shape[0]
    blocks = cells // LANES
    rows = source.shape[0] // 2
    inv = [inverse[(b - 1) % (blocks + 2) : (b - 1) % (blocks + 2) + 1] for b in range(blocks + 2)]
    left = [lhs(v[...]) for v in vectors]
    wide = 2 * LANES
    src = []
    for b in range(0, cells, wide):
        total = source[:, b : b + wide]
        for a, g in zip(left, greens):
            total = total + dot(a, planes(g, b, wide), ((1,), (1,)))
        src += [total[:, :LANES], total[:, LANES:]]
    zero = jnp.zeros((2 * rows, LANES), BF16)

    def sums(u):
        out = []
        for c in range(0, blocks + 2, 2):
            lo, hi = max(c - 1, 0), min(c + 3, blocks + 2)
            window = jnp.concatenate(u[lo:hi], axis=1)
            total = dot(window, hood[(lo - c + 1) * LANES : (hi - c + 1) * LANES])
            out += [total[:, :LANES], total[:, LANES:]]
        return out

    def solved(n):
        out = []
        for b in range(blocks + 2):
            value = src[b - 1] + n[b] if 0 < b <= blocks else n[b]
            out.append((value * inv[b]).astype(BF16))
        return out

    first = [zero] + [(src[b] * inv[b + 1]).astype(BF16) for b in range(blocks)] + [zero]
    slip = solved(sums(solved(sums(first))))
    data = dot(jnp.concatenate(slip[1:-1], axis=1), operator[...])
    odd = lax.rem(part, 2) == 1
    near, far = planes(facing.at[1], 0, REACH), planes(other, 0, REACH)
    low, high = jnp.where(odd, near, far), jnp.where(odd, far, near)
    pad = jnp.zeros((LANES - REACH, wide), BF16)
    data = data + dot(slip[0], jnp.concatenate([pad, low], axis=0))
    data = data + dot(slip[-1], jnp.concatenate([high, pad], axis=0))
    real = weight[...] * (data[:rows, :LANES] - data[rows:, LANES:])
    imag = weight[...] * (data[rows:, :LANES] + data[:rows, LANES:])
    half = rows // 2
    keep[0], keep[1] = real[:half], imag[:half]
    send[0], send[1] = real[half:].astype(BF16), imag[half:].astype(BF16)


def shards(probes, green_blocks, noise_table, station_class, kappa_table, coeff_index):
    nfreq, ngroup = noise_table.shape
    nsens = lax.axis_size("sens")
    sensors, rows_dev = probes.shape[1:]
    cells = green_blocks.shape[1]
    par = lax.axis_index("par")
    odd = par // nfreq % 2 == 1
    vector = jnp.transpose(probes, (0, 2, 1))

    greens = [turned(green_blocks, "sens", k) for k in range(1, nsens)]
    partner = swapped(vector, "par", 2 * nfreq)

    variances = lax.dynamic_index_in_dim(noise_table, par % nfreq, 0)
    member = station_class[None, :] == jnp.arange(ngroup, dtype=jnp.int32)[:, None]
    variance = jnp.sum(jnp.where(member, variances.reshape(ngroup, 1), 0.0), axis=0, keepdims=True)
    weight = 1.0 / jnp.sqrt(variance)

    first, last = green_blocks[:, :REACH], green_blocks[:, -REACH:]
    facing, other = jnp.where(odd, first, last), jnp.where(odd, last, first)

    mine = jnp.stack([vector, partner])
    sent = jnp.stack([mine.reshape(2, -1, sensors), facing])
    got = swapped(sent, "par", nfreq)
    other = crossed(other, "par", nfreq)
    raw = jnp.concatenate([mine, got[0].reshape(mine.shape)], axis=0)
    vectors = (weight[None, None] * raw.astype(F32)).astype(BF16)
    rest = [turned(vectors, "sens", k) for k in range(1, nsens)]

    smem = pl.BlockSpec(memory_space=pltpu.SMEM)
    vmem = pl.BlockSpec(memory_space=pltpu.VMEM)
    rows = SPLIT * rows_dev
    operator, source, inverse, hood = pl.pallas_call(
        functools.partial(own_kernel, nfreq, kappa_table.shape[0]),
        out_shape=[
            jax.ShapeDtypeStruct((cells, 2 * sensors), BF16),
            jax.ShapeDtypeStruct((2 * rows, cells), F32),
            jax.ShapeDtypeStruct((cells // LANES + 2, LANES), F32),
            jax.ShapeDtypeStruct((4 * LANES, 2 * LANES), BF16),
        ],
        in_specs=[smem] + [vmem] * 3,
        out_specs=[vmem] * 4,
        compiler_params=PARAMS,
        name="own",
    )(kappa_table, coeff_index.reshape(-1, LANES), vectors, green_blocks)
    keep, send = pl.pallas_call(
        functools.partial(slip_kernel, nfreq, nsens),
        out_shape=[
            jax.ShapeDtypeStruct((2, rows // 2, sensors), F32),
            jax.ShapeDtypeStruct((2, rows // 2, sensors), BF16),
        ],
        in_specs=[vmem] * (5 + 2 * nsens),
        out_specs=[vmem] * 2,
        compiler_params=PARAMS,
        name="slip",
    )(weight, inverse, hood, source, operator, got, other, *rest, *greens)
    near = keep + swapped(send, "par", nfreq).astype(F32)
    far = swapped(near[:, rows_dev:].astype(BF16), "par", 2 * nfreq)
    return jnp.transpose(near[:, :rows_dev] + far.astype(F32), (0, 2, 1))


def solution(mesh):
    in_specs = (P(None, "sens", "par"), P(None, "par", "sens"), P(), P("sens"), P(), P())
    out_specs = P(None, "sens", "par")
    return jax.shard_map(shards, mesh=mesh, in_specs=in_specs, out_specs=out_specs, check_vma=False)
```

```python
import functools

import jax
import jax.numpy as jnp
from jax import lax
from jax.experimental import pallas as pl
from jax.experimental.pallas import tpu as pltpu
from jax.sharding import PartitionSpec as P

SPLIT = 4
DIP = 32
LANES = 128
REACH = 2 * DIP
F32 = jnp.float32
BF16 = jnp.bfloat16
PRIOR = pl.CostEstimate(flops=1, bytes_accessed=1, transcendentals=0)
BESIDE = pl.CostEstimate(flops=575_000_000, bytes_accessed=1, transcendentals=0)
PARAMS = pltpu.CompilerParams(vmem_limit_bytes=32 * 2**20)


def swapped(value, axis, mask):
    return lax.ppermute(value, axis, [(i, i ^ mask) for i in range(lax.axis_size(axis))])


def turned(value, axis, step):
    size = lax.axis_size(axis)
    return lax.ppermute(value, axis, [(i, (i + step) % size) for i in range(size)])


def crossed(value, axis, nfreq):
    pairs = [(p * nfreq + f, (p + 1) * nfreq + f) for p in range(1, SPLIT - 1, 2) for f in range(nfreq)]
    return lax.ppermute(value, axis, pairs + [(b, a) for a, b in pairs])


def dot(a, b, form=((1,), (0,))):
    return lax.dot_general(a, b, (form, ((), ())), preferred_element_type=F32)


def chosen(table, index, count, place):
    value = jnp.zeros(index.shape, F32)
    for k in range(count):
        value = jnp.where(index == k, place(table, k), value)
    return value


def stencil():
    row = lax.broadcasted_iota(jnp.int32, (4 * LANES, 2 * LANES), 0)
    col = lax.broadcasted_iota(jnp.int32, (4 * LANES, 2 * LANES), 1)
    away = row - LANES - col
    dip = lax.rem(col, DIP)
    hit = (away == DIP) | (away == -DIP)
    hit = hit | ((away == 1) & (dip != DIP - 1)) | ((away == -1) & (dip != 0))
    return hit.astype(F32).astype(BF16)


def planes(ref, b, n):
    return jnp.concatenate([ref[0, b : b + n], ref[1, b : b + n]], axis=1)


def lhs(z):
    rows = z.shape[0] * z.shape[2]
    zr, zi = z[:, 0].reshape(rows, LANES), z[:, 1].reshape(rows, LANES)
    top = jnp.concatenate([zr, zi], axis=1)
    return jnp.concatenate([top, jnp.concatenate([zi, -zr], axis=1)], axis=0)


def prep_kernel(nfreq, noise, station, vector, green, weight, held, facing, other):
    par = lax.axis_index("par")
    freq, part = lax.rem(par, nfreq), lax.div(par, nfreq)
    odd = lax.rem(part, 2)
    cells = green.shape[1]
    first = pl.multiple_of(odd * (cells - REACH), REACH)
    last = pl.multiple_of((1 - odd) * (cells - REACH), REACH)
    held[...] = vector[...]
    facing[...] = green[:, pl.ds(last, REACH)]
    other[...] = green[:, pl.ds(first, REACH)]
    variance = chosen(noise, station[...], noise.shape[1], lambda t, k: t[freq, k])
    weight[...] = 1.0 / jnp.sqrt(variance)


def own_kernel(nfreq, nclass, kappa, coeff, vector, green, facing, other, operator, rims, source, inverse, hood):
    part = lax.div(lax.axis_index("par"), nfreq)
    cells = green.shape[1]
    blocks = cells // LANES
    parts = coeff.shape[0] // blocks

    def inv(index):
        return 1.0 / (4.0 + chosen(kappa, index, nclass, lambda t, k: t[k]))

    before = inv(coeff[pl.ds(jnp.maximum(part * blocks - 1, 0), 1), :])
    after = inv(coeff[pl.ds(jnp.minimum((part + 1) * blocks, parts * blocks - 1), 1), :])
    inverse[0:blocks, :] = inv(coeff[pl.ds(part * blocks, blocks), :])
    inverse[blocks : blocks + 1, :] = jnp.where(part < parts - 1, after, 0.0)
    inverse[blocks + 1 : blocks + 2, :] = jnp.where(part > 0, before, 0.0)
    hood[...] = stencil()
    odd = lax.rem(part, 2) == 1
    near, far = planes(facing.at[1], 0, REACH), planes(other, 0, REACH)
    rims[0], rims[1] = jnp.where(odd, far, near), jnp.where(odd, near, far)
    both = planes(green, 0, cells)
    operator[...] = both
    source[...] = dot(lhs(vector[...]), both, ((1,), (1,)))


def slip_kernel(nsens, weight, inverse, hood, source, operator, rims, *refs):
    vectors, refs = refs[: nsens - 1], refs[nsens - 1 :]
    greens, (keep, send) = refs[: nsens - 1], refs[nsens - 1 :]
    cells = operator.shape[0]
    blocks = cells // LANES
    rows = source.shape[0] // 2
    inv = [inverse[(b - 1) % (blocks + 2) : (b - 1) % (blocks + 2) + 1] for b in range(blocks + 2)]
    left = [lhs(v[...]) for v in vectors]
    wide = 2 * LANES
    src = []
    for b in range(0, cells, wide):
        total = source[:, b : b + wide]
        for a, g in zip(left, greens):
            total = total + dot(a, planes(g, b, wide), ((1,), (1,)))
        src += [total[:, :LANES], total[:, LANES:]]
    zero = jnp.zeros((2 * rows, LANES), BF16)

    def sums(u):
        out = []
        for c in range(0, blocks + 2, 2):
            lo, hi = max(c - 1, 0), min(c + 3, blocks + 2)
            window = jnp.concatenate(u[lo:hi], axis=1)
            total = dot(window, hood[(lo - c + 1) * LANES : (hi - c + 1) * LANES])
            out += [total[:, :LANES], total[:, LANES:]]
        return out

    def solved(n):
        out = []
        for b in range(blocks + 2):
            value = src[b - 1] + n[b] if 0 < b <= blocks else n[b]
            out.append((value * inv[b]).astype(BF16))
        return out

    first = [zero] + [(src[b] * inv[b + 1]).astype(BF16) for b in range(blocks)] + [zero]
    slip = solved(sums(solved(sums(first))))
    data = dot(jnp.concatenate(slip[1:-1], axis=1), operator[...])
    pad = jnp.zeros((LANES - REACH, wide), BF16)
    data = data + dot(slip[0], jnp.concatenate([pad, rims[1]], axis=0))
    data = data + dot(slip[-1], jnp.concatenate([rims[0], pad], axis=0))
    real = weight[...] * (data[:rows, :LANES] - data[rows:, LANES:])
    imag = weight[...] * (data[rows:, :LANES] + data[:rows, LANES:])
    half = rows // 2
    keep[0], keep[1] = real[:half], imag[:half]
    send[0], send[1] = real[half:].astype(BF16), imag[half:].astype(BF16)


def shards(probes, green_blocks, noise_table, station_class, kappa_table, coeff_index):
    nfreq = noise_table.shape[0]
    nsens = lax.axis_size("sens")
    sensors, rows_dev = probes.shape[1:]
    cells = green_blocks.shape[1]
    smem = pl.BlockSpec(memory_space=pltpu.SMEM)
    vmem = pl.BlockSpec(memory_space=pltpu.VMEM)
    greens = [turned(green_blocks, "sens", k) for k in range(1, nsens)]
    vector = jnp.transpose(probes, (0, 2, 1))
    partner = swapped(vector, "par", 2 * nfreq)

    rim = jax.ShapeDtypeStruct((2, REACH, sensors), BF16)
    weight, held, facing, other = pl.pallas_call(
        functools.partial(prep_kernel, nfreq),
        out_shape=[
            jax.ShapeDtypeStruct((1, sensors), F32),
            jax.ShapeDtypeStruct((2, rows_dev, sensors), BF16),
            rim,
            rim,
        ],
        in_specs=[smem] + [vmem] * 3,
        out_specs=[vmem] * 4,
        compiler_params=PARAMS,
        cost_estimate=PRIOR,
        name="prep",
    )(noise_table, station_class.reshape(1, -1), vector, green_blocks)

    mine = jnp.stack([held, partner])
    sent = jnp.stack([mine.reshape(2, -1, sensors), facing])
    got = swapped(sent, "par", nfreq)
    other = crossed(other, "par", nfreq)
    vectors = jnp.concatenate([mine, got[0].reshape(mine.shape)], axis=0)
    vectors = (weight * vectors.astype(F32)).astype(BF16)
    rest = [turned(vectors, "sens", k) for k in range(1, nsens)]
    rows = SPLIT * rows_dev
    operator, rims, source, inverse, hood = pl.pallas_call(
        functools.partial(own_kernel, nfreq, kappa_table.shape[0]),
        out_shape=[
            jax.ShapeDtypeStruct((cells, 2 * sensors), BF16),
            jax.ShapeDtypeStruct((2, REACH, 2 * sensors), BF16),
            jax.ShapeDtypeStruct((2 * rows, cells), F32),
            jax.ShapeDtypeStruct((cells // LANES + 2, LANES), F32),
            jax.ShapeDtypeStruct((4 * LANES, 2 * LANES), BF16),
        ],
        in_specs=[smem] + [vmem] * 5,
        out_specs=[vmem] * 5,
        compiler_params=PARAMS,
        cost_estimate=BESIDE,
        name="own",
    )(kappa_table, coeff_index.reshape(-1, LANES), vectors, green_blocks, got, other)
    keep, send = pl.pallas_call(
        functools.partial(slip_kernel, nsens),
        out_shape=[
            jax.ShapeDtypeStruct((2, rows // 2, sensors), F32),
            jax.ShapeDtypeStruct((2, rows // 2, sensors), BF16),
        ],
        in_specs=[vmem] * (4 + 2 * nsens),
        out_specs=[vmem] * 2,
        compiler_params=PARAMS,
        name="slip",
    )(weight, inverse, hood, source, operator, rims, *rest, *greens)
    near = keep + swapped(send, "par", nfreq).astype(F32)
    far = swapped(near[:, rows_dev:].astype(BF16), "par", 2 * nfreq)
    return jnp.transpose(near[:, :rows_dev] + far.astype(F32), (0, 2, 1))


def solution(mesh):
    in_specs = (P(None, "sens", "par"), P(None, "par", "sens"), P(), P("sens"), P(), P())
    out_specs = P(None, "sens", "par")
    return jax.shard_map(shards, mesh=mesh, in_specs=in_specs, out_specs=out_specs, check_vma=False)
```

```python
import functools

import jax
import jax.numpy as jnp
from jax import lax
from jax.experimental import pallas as pl
from jax.experimental.pallas import tpu as pltpu
from jax.sharding import PartitionSpec as P

SPLIT = 4
DIP = 32
LANES = 128
REACH = 2 * DIP
F32 = jnp.float32
BF16 = jnp.bfloat16
PRIOR = pl.CostEstimate(flops=1, bytes_accessed=1, transcendentals=0)
BESIDE = pl.CostEstimate(flops=575_000_000, bytes_accessed=1, transcendentals=0)
PARAMS = pltpu.CompilerParams(vmem_limit_bytes=32 * 2**20)


def swapped(value, axis, mask):
    return lax.ppermute(value, axis, [(i, i ^ mask) for i in range(lax.axis_size(axis))])


def turned(value, axis, step):
    size = lax.axis_size(axis)
    return lax.ppermute(value, axis, [(i, (i + step) % size) for i in range(size)])


def crossed(value, axis, nfreq):
    pairs = [(p * nfreq + f, (p + 1) * nfreq + f) for p in range(1, SPLIT - 1, 2) for f in range(nfreq)]
    return lax.ppermute(value, axis, pairs + [(b, a) for a, b in pairs])


def dot(a, b, form=((1,), (0,))):
    return lax.dot_general(a, b, (form, ((), ())), preferred_element_type=F32)


def chosen(table, index, count, place):
    value = jnp.zeros(index.shape, F32)
    for k in range(count):
        value = jnp.where(index == k, place(table, k), value)
    return value


def stencil():
    row = lax.broadcasted_iota(jnp.int32, (LANES, LANES + 2 * DIP), 0)
    col = lax.broadcasted_iota(jnp.int32, (LANES, LANES + 2 * DIP), 1)
    away = col - DIP - row
    dip = lax.rem(row, DIP)
    hit = (away == DIP) | (away == -DIP)
    hit = hit | ((away == 1) & (dip != DIP - 1)) | ((away == -1) & (dip != 0))
    return hit.astype(F32).astype(BF16)


def planes(ref, b, n):
    return jnp.concatenate([ref[0, b : b + n], ref[1, b : b + n]], axis=1)


def lhs(z):
    rows = z.shape[0] * z.shape[2]
    zr, zi = z[:, 0].reshape(rows, LANES), z[:, 1].reshape(rows, LANES)
    top = jnp.concatenate([zr, zi], axis=1)
    return jnp.concatenate([top, jnp.concatenate([zi, -zr], axis=1)], axis=0)


def prep_kernel(nfreq, noise, station, vector, green, weight, held, facing, other):
    par = lax.axis_index("par")
    freq, part = lax.rem(par, nfreq), lax.div(par, nfreq)
    odd = lax.rem(part, 2)
    cells = green.shape[1]
    first = pl.multiple_of(odd * (cells - REACH), REACH)
    last = pl.multiple_of((1 - odd) * (cells - REACH), REACH)
    held[...] = vector[...]
    facing[...] = green[:, pl.ds(last, REACH)]
    other[...] = green[:, pl.ds(first, REACH)]
    variance = chosen(noise, station[...], noise.shape[1], lambda t, k: t[freq, k])
    weight[...] = 1.0 / jnp.sqrt(variance)


def gram(swept, operator):
    full = dot(swept, operator)
    real = full[:LANES, :LANES] + full[LANES:, LANES:]
    imag = full[:LANES, LANES:] - full[LANES:, :LANES]
    both = jnp.concatenate([real, imag], axis=1)
    high = both.astype(BF16)
    return high, (both - high.astype(F32)).astype(BF16)


def applied(z, high, low):
    side = lhs(z)
    return dot(side, high, ((1,), (1,))) + dot(side, low, ((1,), (1,)))


def own_kernel(nfreq, nclass, kappa, coeff, vector, green, facing, other, swept, base, operator, inverse, first, second):
    part = lax.div(lax.axis_index("par"), nfreq)
    cells = green.shape[1]
    blocks = cells // LANES
    parts = coeff.shape[0] // blocks
    extent = cells + 2 * REACH

    def column(index, inside):
        value = 1.0 / (4.0 + chosen(kappa, index, nclass, lambda t, k: t[k]))
        value = jnp.where(inside, value, 0.0)
        return jnp.transpose(jnp.broadcast_to(value, (LANES, LANES)))

    before = coeff[pl.ds(jnp.maximum(part * blocks - 1, 0), 1), :]
    after = coeff[pl.ds(jnp.minimum((part + 1) * blocks, parts * blocks - 1), 1), :]
    inverse[0:REACH] = column(before, part > 0)[LANES - REACH :]
    inverse[extent - REACH : extent] = column(after, part < parts - 1)[:REACH]
    for b in range(blocks):
        inverse[REACH + b * LANES : REACH + (b + 1) * LANES] = column(
            coeff[pl.ds(part * blocks + b, 1), :], True
        )

    odd = lax.rem(part, 2) == 1
    near, far = planes(facing.at[1], 0, REACH), planes(other, 0, REACH)
    operator[0:REACH] = jnp.where(odd, near, far)
    operator[REACH : REACH + cells] = planes(green, 0, cells)
    operator[extent - REACH : extent] = jnp.where(odd, far, near)

    hood = stencil()
    none = jnp.zeros((DIP, 2 * LANES), BF16)
    for ref in (first, second):
        ref[0:DIP] = none
        ref[DIP + extent : 2 * DIP + extent] = none

    def solved(at, value):
        scale = inverse[at : at + LANES]
        return jnp.concatenate([scale, scale], axis=1) * value

    for at in range(0, extent, LANES):
        value = solved(at, operator[at : at + LANES].astype(F32))
        first[DIP + at : DIP + at + LANES] = value.astype(BF16)
    for at in range(0, extent, LANES):
        total = operator[at : at + LANES].astype(F32) + dot(hood, first[at : at + LANES + 2 * DIP])
        second[DIP + at : DIP + at + LANES] = solved(at, total).astype(BF16)
    for at in range(REACH, REACH + cells, LANES):
        total = operator[at : at + LANES].astype(F32) + dot(hood, second[at : at + LANES + 2 * DIP])
        swept[:, at - REACH : at - REACH + LANES] = jnp.transpose(solved(at, total)).astype(BF16)
    high, low = gram(swept[...], operator[REACH : REACH + cells])
    base[...] = applied(vector[...], high, low)


def cross_kernel(swept, green, pair):
    pair[0], pair[1] = gram(swept[...], planes(green, 0, green.shape[1]))


def data_kernel(nsens, weight, base, *refs):
    vectors, pairs, (keep, send) = refs[: nsens - 1], refs[nsens - 1 : 2 * nsens - 2], refs[2 * nsens - 2 :]
    data = base[...]
    for v, p in zip(vectors, pairs):
        data = data + applied(v[...], p[0], p[1])
    data = weight[...] * data
    half = data.shape[0] // 4
    for k in range(2):
        keep[k] = data[2 * k * half : (2 * k + 1) * half]
        send[k] = data[(2 * k + 1) * half : (2 * k + 2) * half].astype(BF16)


def shards(probes, green_blocks, noise_table, station_class, kappa_table, coeff_index):
    nfreq = noise_table.shape[0]
    nsens = lax.axis_size("sens")
    sensors, rows_dev = probes.shape[1:]
    cells = green_blocks.shape[1]
    smem = pl.BlockSpec(memory_space=pltpu.SMEM)
    vmem = pl.BlockSpec(memory_space=pltpu.VMEM)
    greens = [turned(green_blocks, "sens", k) for k in range(1, nsens)]
    vector = jnp.transpose(probes, (0, 2, 1))
    partner = swapped(vector, "par", 2 * nfreq)

    rim = jax.ShapeDtypeStruct((2, REACH, sensors), BF16)
    weight, held, facing, other = pl.pallas_call(
        functools.partial(prep_kernel, nfreq),
        out_shape=[
            jax.ShapeDtypeStruct((1, sensors), F32),
            jax.ShapeDtypeStruct((2, rows_dev, sensors), BF16),
            rim,
            rim,
        ],
        in_specs=[smem] + [vmem] * 3,
        out_specs=[vmem] * 4,
        compiler_params=PARAMS,
        cost_estimate=PRIOR,
        name="prep",
    )(noise_table, station_class.reshape(1, -1), vector, green_blocks)

    mine = jnp.stack([held, partner])
    sent = jnp.stack([mine.reshape(2, -1, sensors), facing])
    got = swapped(sent, "par", nfreq)
    other = crossed(other, "par", nfreq)
    vectors = jnp.concatenate([mine, got[0].reshape(mine.shape)], axis=0)
    vectors = (weight * vectors.astype(F32)).astype(BF16)
    rest = [turned(vectors, "sens", k) for k in range(1, nsens)]
    rows = SPLIT * rows_dev
    extent = cells + 2 * REACH
    swept, base = pl.pallas_call(
        functools.partial(own_kernel, nfreq, kappa_table.shape[0]),
        out_shape=[
            jax.ShapeDtypeStruct((2 * sensors, cells), BF16),
            jax.ShapeDtypeStruct((2 * rows, sensors), F32),
        ],
        in_specs=[smem] + [vmem] * 5,
        out_specs=[vmem] * 2,
        scratch_shapes=[
            pltpu.VMEM((extent, 2 * sensors), BF16),
            pltpu.VMEM((extent, LANES), F32),
            pltpu.VMEM((extent + 2 * DIP, 2 * sensors), BF16),
            pltpu.VMEM((extent + 2 * DIP, 2 * sensors), BF16),
        ],
        compiler_params=PARAMS,
        cost_estimate=BESIDE,
        name="own",
    )(kappa_table, coeff_index.reshape(-1, LANES), vectors, green_blocks, got, other)
    pairs = [
        pl.pallas_call(
            cross_kernel,
            out_shape=jax.ShapeDtypeStruct((2, sensors, 2 * sensors), BF16),
            in_specs=[vmem] * 2,
            out_specs=vmem,
            compiler_params=PARAMS,
            cost_estimate=PRIOR,
            name="cross",
        )(swept, g)
        for g in greens
    ]
    keep, send = pl.pallas_call(
        functools.partial(data_kernel, nsens),
        out_shape=[
            jax.ShapeDtypeStruct((2, rows // 2, sensors), F32),
            jax.ShapeDtypeStruct((2, rows // 2, sensors), BF16),
        ],
        in_specs=[vmem] * (2 * nsens),
        out_specs=[vmem] * 2,
        compiler_params=PARAMS,
        name="data",
    )(weight, base, *rest, *pairs)
    near = keep + swapped(send, "par", nfreq).astype(F32)
    far = swapped(near[:, rows_dev:].astype(BF16), "par", 2 * nfreq)
    return jnp.transpose(near[:, :rows_dev] + far.astype(F32), (0, 2, 1))


def solution(mesh):
    in_specs = (P(None, "sens", "par"), P(None, "par", "sens"), P(), P("sens"), P(), P())
    out_specs = P(None, "sens", "par")
    return jax.shard_map(shards, mesh=mesh, in_specs=in_specs, out_specs=out_specs, check_vma=False)
```

```python
import functools

import jax
import jax.numpy as jnp
from jax import lax
from jax.experimental import pallas as pl
from jax.experimental.pallas import tpu as pltpu
from jax.sharding import PartitionSpec as P

SPLIT = 4
DIP = 32
LANES = 128
REACH = 2 * DIP
F32 = jnp.float32
BF16 = jnp.bfloat16
PRIOR = pl.CostEstimate(flops=1, bytes_accessed=1, transcendentals=0)
BESIDE = pl.CostEstimate(flops=575_000_000, bytes_accessed=1, transcendentals=0)
PARAMS = pltpu.CompilerParams(vmem_limit_bytes=32 * 2**20)


def swapped(value, axis, mask):
    return lax.ppermute(value, axis, [(i, i ^ mask) for i in range(lax.axis_size(axis))])


def turned(value, axis, step):
    size = lax.axis_size(axis)
    return lax.ppermute(value, axis, [(i, (i + step) % size) for i in range(size)])


def crossed(value, axis, nfreq):
    pairs = []
    for i in range(lax.axis_size(axis)):
        part = i // nfreq
        outer = part in (0, SPLIT - 1)
        pairs.append((i, i ^ 1 if outer else i + nfreq if part % 2 else i - nfreq))
    return lax.ppermute(value, axis, pairs)


def dot(a, b, form=((1,), (0,))):
    return lax.dot_general(a, b, (form, ((), ())), preferred_element_type=F32)


def chosen(table, index, count, place):
    value = jnp.zeros(index.shape, F32)
    for k in range(count):
        value = jnp.where(index == k, place(table, k), value)
    return value


def stencil():
    row = lax.broadcasted_iota(jnp.int32, (LANES, LANES + 2 * DIP), 0)
    col = lax.broadcasted_iota(jnp.int32, (LANES, LANES + 2 * DIP), 1)
    away = col - DIP - row
    dip = lax.rem(row, DIP)
    hit = (away == DIP) | (away == -DIP)
    hit = hit | ((away == 1) & (dip != DIP - 1)) | ((away == -1) & (dip != 0))
    return hit.astype(F32).astype(BF16)


def planes(ref, b, n):
    return jnp.concatenate([ref[0, b : b + n], ref[1, b : b + n]], axis=1)


def lhs(z):
    rows = z.shape[0] * z.shape[2]
    zr, zi = z[:, 0].reshape(rows, LANES), z[:, 1].reshape(rows, LANES)
    top = jnp.concatenate([zr, zi], axis=1)
    return jnp.concatenate([top, jnp.concatenate([zi, -zr], axis=1)], axis=0)


def prep_kernel(nfreq, noise, station, vector, green, weight, held, facing, other):
    par = lax.axis_index("par")
    freq, part = lax.rem(par, nfreq), lax.div(par, nfreq)
    odd = lax.rem(part, 2)
    cells = green.shape[1]
    first = pl.multiple_of(odd * (cells - REACH), REACH)
    last = pl.multiple_of((1 - odd) * (cells - REACH), REACH)
    held[...] = vector[...]
    facing[...] = green[:, pl.ds(last, REACH)]
    other[...] = green[:, pl.ds(first, REACH)]
    variance = chosen(noise, station[...], noise.shape[1], lambda t, k: t[freq, k])
    weight[...] = 1.0 / jnp.sqrt(variance)


def gram(swept, operator):
    full = dot(swept, operator)
    real = full[:LANES, :LANES] + full[LANES:, LANES:]
    imag = full[:LANES, LANES:] - full[LANES:, :LANES]
    both = jnp.concatenate([real, imag], axis=1)
    high = both.astype(BF16)
    return high, (both - high.astype(F32)).astype(BF16)


def applied(z, high, low):
    side = lhs(z)
    return dot(side, high, ((1,), (1,))) + dot(side, low, ((1,), (1,)))


def own_kernel(nfreq, nclass, kappa, coeff, vector, green, facing, other, swept, base, operator, inverse, first, second):
    part = lax.div(lax.axis_index("par"), nfreq)
    cells = green.shape[1]
    blocks = cells // LANES
    parts = coeff.shape[0] // blocks
    extent = cells + 2 * REACH

    def inv(index):
        return 1.0 / (4.0 + chosen(kappa, index, nclass, lambda t, k: t[k]))

    def column(value):
        return jnp.transpose(jnp.broadcast_to(value, (LANES, LANES)))

    before = inv(coeff[pl.ds(jnp.maximum(part * blocks - 1, 0), 1), :])
    after = inv(coeff[pl.ds(jnp.minimum((part + 1) * blocks, parts * blocks - 1), 1), :])
    inside = inv(coeff[pl.ds(pl.multiple_of(part * blocks, blocks), blocks), :])
    inverse[0:REACH] = column(jnp.where(part > 0, before, 0.0))[LANES - REACH :]
    inverse[extent - REACH : extent] = column(jnp.where(part < parts - 1, after, 0.0))[:REACH]
    for b in range(blocks):
        inverse[REACH + b * LANES : REACH + (b + 1) * LANES] = column(inside[b : b + 1])

    odd = lax.rem(part, 2) == 1
    near, far = planes(facing.at[1], 0, REACH), planes(other, 0, REACH)
    operator[0:REACH] = jnp.where(odd, near, far)
    operator[REACH : REACH + cells] = planes(green, 0, cells)
    operator[extent - REACH : extent] = jnp.where(odd, far, near)

    hood = stencil()
    none = jnp.zeros((DIP, 2 * LANES), BF16)
    for ref in (first, second):
        ref[0:DIP] = none
        ref[DIP + extent : 2 * DIP + extent] = none

    def solved(at, value):
        scale = inverse[at : at + LANES]
        return jnp.concatenate([scale, scale], axis=1) * value

    for at in range(0, extent, LANES):
        value = solved(at, operator[at : at + LANES].astype(F32))
        first[DIP + at : DIP + at + LANES] = value.astype(BF16)
    for at in range(0, extent, LANES):
        total = operator[at : at + LANES].astype(F32) + dot(hood, first[at : at + LANES + 2 * DIP])
        second[DIP + at : DIP + at + LANES] = solved(at, total).astype(BF16)
    for at in range(REACH, REACH + cells, LANES):
        total = operator[at : at + LANES].astype(F32) + dot(hood, second[at : at + LANES + 2 * DIP])
        swept[:, at - REACH : at - REACH + LANES] = jnp.transpose(solved(at, total)).astype(BF16)
    high, low = gram(swept[...], operator[REACH : REACH + cells])
    base[...] = applied(vector[...], high, low)


def cross_kernel(swept, green, pair):
    pair[0], pair[1] = gram(swept[...], planes(green, 0, green.shape[1]))


def data_kernel(nsens, weight, base, *refs):
    vectors, pairs, (keep, send) = refs[: nsens - 1], refs[nsens - 1 : 2 * nsens - 2], refs[2 * nsens - 2 :]
    data = base[...]
    for v, p in zip(vectors, pairs):
        data = data + applied(v[...], p[0], p[1])
    data = weight[...] * data
    half = data.shape[0] // 4
    for k in range(2):
        keep[k] = data[2 * k * half : (2 * k + 1) * half]
        send[k] = data[(2 * k + 1) * half : (2 * k + 2) * half].astype(BF16)


def shards(probes, green_blocks, noise_table, station_class, kappa_table, coeff_index):
    nfreq = noise_table.shape[0]
    nsens = lax.axis_size("sens")
    sensors, rows_dev = probes.shape[1:]
    cells = green_blocks.shape[1]
    smem = pl.BlockSpec(memory_space=pltpu.SMEM)
    vmem = pl.BlockSpec(memory_space=pltpu.VMEM)
    greens = [turned(green_blocks, "sens", k) for k in range(1, nsens)]
    vector = jnp.transpose(probes, (0, 2, 1))
    partner = swapped(vector, "par", 2 * nfreq)

    rim = jax.ShapeDtypeStruct((2, REACH, sensors), BF16)
    weight, held, facing, other = pl.pallas_call(
        functools.partial(prep_kernel, nfreq),
        out_shape=[
            jax.ShapeDtypeStruct((1, sensors), F32),
            jax.ShapeDtypeStruct((2, rows_dev, sensors), BF16),
            rim,
            rim,
        ],
        in_specs=[smem] + [vmem] * 3,
        out_specs=[vmem] * 4,
        compiler_params=PARAMS,
        cost_estimate=PRIOR,
        name="prep",
    )(noise_table, station_class.reshape(1, -1), vector, green_blocks)

    mine = jnp.stack([held, partner])
    sent = jnp.stack([mine.reshape(2, -1, sensors), facing])
    got = swapped(sent, "par", nfreq)
    other = crossed(other, "par", nfreq)
    vectors = jnp.concatenate([mine, got[0].reshape(mine.shape)], axis=0)
    vectors = (weight * vectors.astype(F32)).astype(BF16)
    rest = [turned(vectors, "sens", k) for k in range(1, nsens)]
    rows = SPLIT * rows_dev
    extent = cells + 2 * REACH
    swept, base = pl.pallas_call(
        functools.partial(own_kernel, nfreq, kappa_table.shape[0]),
        out_shape=[
            jax.ShapeDtypeStruct((2 * sensors, cells), BF16),
            jax.ShapeDtypeStruct((2 * rows, sensors), F32),
        ],
        in_specs=[smem] + [vmem] * 5,
        out_specs=[vmem] * 2,
        scratch_shapes=[
            pltpu.VMEM((extent, 2 * sensors), BF16),
            pltpu.VMEM((extent, LANES), F32),
            pltpu.VMEM((extent + 2 * DIP, 2 * sensors), BF16),
            pltpu.VMEM((extent + 2 * DIP, 2 * sensors), BF16),
        ],
        compiler_params=PARAMS,
        cost_estimate=BESIDE,
        name="own",
    )(kappa_table, coeff_index.reshape(-1, LANES), vectors, green_blocks, got, other)
    pairs = [
        pl.pallas_call(
            cross_kernel,
            out_shape=jax.ShapeDtypeStruct((2, sensors, 2 * sensors), BF16),
            in_specs=[vmem] * 2,
            out_specs=vmem,
            compiler_params=PARAMS,
            cost_estimate=PRIOR,
            name="cross",
        )(swept, g)
        for g in greens
    ]
    keep, send = pl.pallas_call(
        functools.partial(data_kernel, nsens),
        out_shape=[
            jax.ShapeDtypeStruct((2, rows // 2, sensors), F32),
            jax.ShapeDtypeStruct((2, rows // 2, sensors), BF16),
        ],
        in_specs=[vmem] * (2 * nsens),
        out_specs=[vmem] * 2,
        compiler_params=PARAMS,
        name="data",
    )(weight, base, *rest, *pairs)
    near = keep + swapped(send, "par", nfreq).astype(F32)
    far = swapped(near[:, rows_dev:].astype(BF16), "par", 2 * nfreq)
    return jnp.transpose(near[:, :rows_dev] + far.astype(F32), (0, 2, 1))


def solution(mesh):
    in_specs = (P(None, "sens", "par"), P(None, "par", "sens"), P(), P("sens"), P(), P())
    out_specs = P(None, "sens", "par")
    return jax.shard_map(shards, mesh=mesh, in_specs=in_specs, out_specs=out_specs, check_vma=False)
```

```python
import functools

import jax
import jax.numpy as jnp
from jax import lax
from jax.experimental import pallas as pl
from jax.experimental.pallas import tpu as pltpu
from jax.sharding import PartitionSpec as P

SPLIT = 4
DIP = 32
LANES = 128
ROUTES = ((1, 3, 2, 0), (2, 1, 0, 3), (3, 0, 1, 2), (0, 2, 3, 1))
PLACE = (0, 2, 1, 3)
REACH = 2 * DIP
F32 = jnp.float32
BF16 = jnp.bfloat16
PRIOR = pl.CostEstimate(flops=1, bytes_accessed=1, transcendentals=0)
BESIDE = pl.CostEstimate(flops=575_000_000, bytes_accessed=1, transcendentals=0)
PARAMS = pltpu.CompilerParams(vmem_limit_bytes=32 * 2**20)


def swapped(value, axis, mask):
    return lax.ppermute(value, axis, [(i, i ^ mask) for i in range(lax.axis_size(axis))])


def turned(value, axis, step):
    size = lax.axis_size(axis)
    return lax.ppermute(value, axis, [(i, (i + step) % size) for i in range(size)])


def crossed(value, axis, nfreq):
    pairs = []
    for i in range(lax.axis_size(axis)):
        part = i // nfreq
        outer = part in (0, SPLIT - 1)
        pairs.append((i, i ^ 1 if outer else i + nfreq if part % 2 else i - nfreq))
    return lax.ppermute(value, axis, pairs)


def routed(value, axis, nfreq, route):
    pairs = []
    for i in range(lax.axis_size(axis)):
        part = i // nfreq
        pairs.append((i, i + (route[part] - part) * nfreq if route[part] != part else i ^ 1))
    return lax.ppermute(value, axis, pairs)


def dot(a, b, form=((1,), (0,))):
    return lax.dot_general(a, b, (form, ((), ())), preferred_element_type=F32)


def chosen(table, index, count, place):
    value = jnp.zeros(index.shape, F32)
    for k in range(count):
        value = jnp.where(index == k, place(table, k), value)
    return value


def stencil():
    row = lax.broadcasted_iota(jnp.int32, (LANES, LANES + 2 * DIP), 0)
    col = lax.broadcasted_iota(jnp.int32, (LANES, LANES + 2 * DIP), 1)
    away = col - DIP - row
    dip = lax.rem(row, DIP)
    hit = (away == DIP) | (away == -DIP)
    hit = hit | ((away == 1) & (dip != DIP - 1)) | ((away == -1) & (dip != 0))
    return hit.astype(F32).astype(BF16)


def planes(ref, b, n):
    return jnp.concatenate([ref[0, b : b + n], ref[1, b : b + n]], axis=1)


def lhs(z):
    rows = z.shape[0] * z.shape[2]
    zr, zi = z[:, 0].reshape(rows, LANES), z[:, 1].reshape(rows, LANES)
    top = jnp.concatenate([zr, zi], axis=1)
    return jnp.concatenate([top, jnp.concatenate([zi, -zr], axis=1)], axis=0)


def prep_kernel(nfreq, noise, station, vector, green, weight, held, facing, other):
    par = lax.axis_index("par")
    freq, part = lax.rem(par, nfreq), lax.div(par, nfreq)
    odd = lax.rem(part, 2)
    cells = green.shape[1]
    first = pl.multiple_of(odd * (cells - REACH), REACH)
    last = pl.multiple_of((1 - odd) * (cells - REACH), REACH)
    held[...] = vector[...]
    facing[...] = green[:, pl.ds(last, REACH)]
    other[...] = green[:, pl.ds(first, REACH)]
    variance = chosen(noise, station[...], noise.shape[1], lambda t, k: t[freq, k])
    weight[...] = 1.0 / jnp.sqrt(variance)


def gram(swept, operator):
    full = dot(swept, operator)
    real = full[:LANES, :LANES] + full[LANES:, LANES:]
    imag = full[:LANES, LANES:] - full[LANES:, :LANES]
    both = jnp.concatenate([real, imag], axis=1)
    high = both.astype(BF16)
    return high, (both - high.astype(F32)).astype(BF16)


def applied(z, high, low):
    side = lhs(z)
    return dot(side, high, ((1,), (1,))) + dot(side, low, ((1,), (1,)))


def own_kernel(nfreq, nclass, kappa, coeff, vector, green, facing, other, swept, base, operator, inverse, first, second):
    part = lax.div(lax.axis_index("par"), nfreq)
    cells = green.shape[1]
    blocks = cells // LANES
    parts = coeff.shape[0] // blocks
    extent = cells + 2 * REACH

    def inv(index):
        return 1.0 / (4.0 + chosen(kappa, index, nclass, lambda t, k: t[k]))

    def column(value):
        return jnp.transpose(jnp.broadcast_to(value, (LANES, LANES)))

    before = inv(coeff[pl.ds(jnp.maximum(part * blocks - 1, 0), 1), :])
    after = inv(coeff[pl.ds(jnp.minimum((part + 1) * blocks, parts * blocks - 1), 1), :])
    inside = inv(coeff[pl.ds(pl.multiple_of(part * blocks, blocks), blocks), :])
    inverse[0:REACH] = column(jnp.where(part > 0, before, 0.0))[LANES - REACH :]
    inverse[extent - REACH : extent] = column(jnp.where(part < parts - 1, after, 0.0))[:REACH]
    for b in range(blocks):
        inverse[REACH + b * LANES : REACH + (b + 1) * LANES] = column(inside[b : b + 1])

    odd = lax.rem(part, 2) == 1
    near, far = planes(facing.at[1], 0, REACH), planes(other, 0, REACH)
    operator[0:REACH] = jnp.where(odd, near, far)
    operator[REACH : REACH + cells] = planes(green, 0, cells)
    operator[extent - REACH : extent] = jnp.where(odd, far, near)

    hood = stencil()
    none = jnp.zeros((DIP, 2 * LANES), BF16)
    for ref in (first, second):
        ref[0:DIP] = none
        ref[DIP + extent : 2 * DIP + extent] = none

    def solved(at, value):
        scale = inverse[at : at + LANES]
        return jnp.concatenate([scale, scale], axis=1) * value

    for at in range(0, extent, LANES):
        value = solved(at, operator[at : at + LANES].astype(F32))
        first[DIP + at : DIP + at + LANES] = value.astype(BF16)
    for at in range(0, extent, LANES):
        total = operator[at : at + LANES].astype(F32) + dot(hood, first[at : at + LANES + 2 * DIP])
        second[DIP + at : DIP + at + LANES] = solved(at, total).astype(BF16)
    for at in range(REACH, REACH + cells, LANES):
        total = operator[at : at + LANES].astype(F32) + dot(hood, second[at : at + LANES + 2 * DIP])
        swept[:, at - REACH : at - REACH + LANES] = jnp.transpose(solved(at, total)).astype(BF16)
    high, low = gram(swept[...], operator[REACH : REACH + cells])
    base[...] = applied(vector[...], high, low)


def cross_kernel(swept, green, pair):
    pair[0], pair[1] = gram(swept[...], planes(green, 0, green.shape[1]))


def data_kernel(nfreq, nsens, weight, base, *refs):
    vectors, pairs, (keep, *sends, total) = refs[: nsens - 1], refs[nsens - 1 : 2 * nsens - 2], refs[2 * nsens - 2 :]
    part = lax.div(lax.axis_index("par"), nfreq)
    data = base[...]
    for v, p in zip(vectors, pairs):
        data = data + applied(v[...], p[0], p[1])
    total[...] = weight[...] * data
    half = data.shape[0] // 2
    rows = half // SPLIT
    for k in range(2):
        keep[k] = total[k * half : k * half + rows]
    for send, route in zip(sends, ROUTES):
        place = sum(jnp.where(part == p, PLACE[p ^ q], 0) for p, q in enumerate(route))
        for k in range(2):
            send[k] = total[pl.ds(pl.multiple_of(k * half + place * rows, rows), rows), :].astype(BF16)


def shards(probes, green_blocks, noise_table, station_class, kappa_table, coeff_index):
    nfreq = noise_table.shape[0]
    nsens = lax.axis_size("sens")
    sensors, rows_dev = probes.shape[1:]
    cells = green_blocks.shape[1]
    smem = pl.BlockSpec(memory_space=pltpu.SMEM)
    vmem = pl.BlockSpec(memory_space=pltpu.VMEM)
    greens = [turned(green_blocks, "sens", k) for k in range(1, nsens)]
    vector = jnp.transpose(probes, (0, 2, 1))
    partner = swapped(vector, "par", 2 * nfreq)

    rim = jax.ShapeDtypeStruct((2, REACH, sensors), BF16)
    weight, held, facing, other = pl.pallas_call(
        functools.partial(prep_kernel, nfreq),
        out_shape=[
            jax.ShapeDtypeStruct((1, sensors), F32),
            jax.ShapeDtypeStruct((2, rows_dev, sensors), BF16),
            rim,
            rim,
        ],
        in_specs=[smem] + [vmem] * 3,
        out_specs=[vmem] * 4,
        compiler_params=PARAMS,
        cost_estimate=PRIOR,
        name="prep",
    )(noise_table, station_class.reshape(1, -1), vector, green_blocks)

    mine = jnp.stack([held, partner])
    sent = jnp.stack([mine.reshape(2, -1, sensors), facing])
    got = swapped(sent, "par", nfreq)
    other = crossed(other, "par", nfreq)
    vectors = jnp.concatenate([mine, got[0].reshape(mine.shape)], axis=0)
    vectors = (weight * vectors.astype(F32)).astype(BF16)
    rest = [turned(vectors, "sens", k) for k in range(1, nsens)]
    rows = SPLIT * rows_dev
    extent = cells + 2 * REACH
    swept, base = pl.pallas_call(
        functools.partial(own_kernel, nfreq, kappa_table.shape[0]),
        out_shape=[
            jax.ShapeDtypeStruct((2 * sensors, cells), BF16),
            jax.ShapeDtypeStruct((2 * rows, sensors), F32),
        ],
        in_specs=[smem] + [vmem] * 5,
        out_specs=[vmem] * 2,
        scratch_shapes=[
            pltpu.VMEM((extent, 2 * sensors), BF16),
            pltpu.VMEM((extent, LANES), F32),
            pltpu.VMEM((extent + 2 * DIP, 2 * sensors), BF16),
            pltpu.VMEM((extent + 2 * DIP, 2 * sensors), BF16),
        ],
        compiler_params=PARAMS,
        cost_estimate=BESIDE,
        name="own",
    )(kappa_table, coeff_index.reshape(-1, LANES), vectors, green_blocks, got, other)
    pairs = [
        pl.pallas_call(
            cross_kernel,
            out_shape=jax.ShapeDtypeStruct((2, sensors, 2 * sensors), BF16),
            in_specs=[vmem] * 2,
            out_specs=vmem,
            compiler_params=PARAMS,
            cost_estimate=PRIOR,
            name="cross",
        )(swept, g)
        for g in greens
    ]
    keep, *sends = pl.pallas_call(
        functools.partial(data_kernel, nfreq, nsens),
        out_shape=[
            jax.ShapeDtypeStruct((2, rows_dev, sensors), dtype) for dtype in [F32] + [BF16] * len(ROUTES)
        ],
        in_specs=[vmem] * (2 * nsens),
        out_specs=[vmem] * (1 + len(ROUTES)),
        scratch_shapes=[pltpu.VMEM((2 * rows, sensors), F32)],
        compiler_params=PARAMS,
        name="data",
    )(weight, base, *rest, *pairs)
    part = lax.axis_index("par") // nfreq
    for route, send in zip(ROUTES, sends):
        share = routed(send, "par", nfreq, route).astype(F32)
        keep = lax.optimization_barrier(keep)
        for p in range(SPLIT):
            if route[p] == p:
                share = jnp.where(part == p, 0.0, share)
        keep = keep + share
    return jnp.transpose(keep, (0, 2, 1))


def solution(mesh):
    in_specs = (P(None, "sens", "par"), P(None, "par", "sens"), P(), P("sens"), P(), P())
    out_specs = P(None, "sens", "par")
    return jax.shard_map(shards, mesh=mesh, in_specs=in_specs, out_specs=out_specs, check_vma=False)
```

```python
import functools

import jax
import jax.numpy as jnp
from jax import lax
from jax.experimental import pallas as pl
from jax.experimental.pallas import tpu as pltpu
from jax.sharding import PartitionSpec as P

SPLIT = 4
DIP = 32
LANES = 128
ROUTES = (((1, 2, 3, 0), (3, 2, 1, 0)), ((-1, -1, 0, -1), (2, -1, -1, -1)), ((3, 0, 1, 2), (1, 3, 0, 2)), ((2, 3, -1, 1), (-1, 0, 3, 1)))
PLACE = (0, 1, 0, 2)
REACH = 2 * DIP
F32 = jnp.float32
BF16 = jnp.bfloat16
PRIOR = pl.CostEstimate(flops=1, bytes_accessed=1, transcendentals=0)
BESIDE = pl.CostEstimate(flops=575_000_000, bytes_accessed=1, transcendentals=0)
PARAMS = pltpu.CompilerParams(vmem_limit_bytes=32 * 2**20)


def swapped(value, axis, mask):
    return lax.ppermute(value, axis, [(i, i ^ mask) for i in range(lax.axis_size(axis))])


def turned(value, axis, step):
    size = lax.axis_size(axis)
    return lax.ppermute(value, axis, [(i, (i + step) % size) for i in range(size)])


def crossed(value, axis, nfreq):
    pairs = []
    for i in range(lax.axis_size(axis)):
        part = i // nfreq
        outer = part in (0, SPLIT - 1)
        pairs.append((i, i ^ 1 if outer else i + nfreq if part % 2 else i - nfreq))
    return lax.ppermute(value, axis, pairs)


def routed(value, axis, nfreq, step):
    pairs = []
    for i in range(lax.axis_size(axis)):
        part, to = i // nfreq, step[i % 2][i // nfreq]
        pairs.append((i, i ^ 1 if to < 0 else i + (to - part) * nfreq))
    return lax.ppermute(value, axis, pairs)


def dot(a, b, form=((1,), (0,))):
    return lax.dot_general(a, b, (form, ((), ())), preferred_element_type=F32)


def chosen(table, index, count, place):
    value = jnp.zeros(index.shape, F32)
    for k in range(count):
        value = jnp.where(index == k, place(table, k), value)
    return value


def stencil():
    row = lax.broadcasted_iota(jnp.int32, (LANES, LANES + 2 * DIP), 0)
    col = lax.broadcasted_iota(jnp.int32, (LANES, LANES + 2 * DIP), 1)
    away = col - DIP - row
    dip = lax.rem(row, DIP)
    hit = (away == DIP) | (away == -DIP)
    hit = hit | ((away == 1) & (dip != DIP - 1)) | ((away == -1) & (dip != 0))
    return hit.astype(F32).astype(BF16)


def planes(ref, b, n):
    return jnp.concatenate([ref[0, b : b + n], ref[1, b : b + n]], axis=1)


def lhs(z):
    rows = z.shape[0] * z.shape[2]
    zr, zi = z[:, 0].reshape(rows, LANES), z[:, 1].reshape(rows, LANES)
    top = jnp.concatenate([zr, zi], axis=1)
    return jnp.concatenate([top, jnp.concatenate([zi, -zr], axis=1)], axis=0)


def prep_kernel(nfreq, noise, station, vector, green, weight, held, facing, other):
    par = lax.axis_index("par")
    freq, part = lax.rem(par, nfreq), lax.div(par, nfreq)
    odd = lax.rem(part, 2)
    cells = green.shape[1]
    first = pl.multiple_of(odd * (cells - REACH), REACH)
    last = pl.multiple_of((1 - odd) * (cells - REACH), REACH)
    held[...] = vector[...]
    facing[...] = green[:, pl.ds(last, REACH)]
    other[...] = green[:, pl.ds(first, REACH)]
    variance = chosen(noise, station[...], noise.shape[1], lambda t, k: t[freq, k])
    weight[...] = 1.0 / jnp.sqrt(variance)


def halves(full):
    real = full[:LANES, :LANES] + full[LANES:, LANES:]
    imag = full[:LANES, LANES:] - full[LANES:, :LANES]
    both = jnp.concatenate([real, imag], axis=1)
    high = both.astype(BF16)
    return high, (both - high.astype(F32)).astype(BF16)


def applied(z, high, low):
    side = lhs(z)
    return dot(side, high, ((1,), (1,))) + dot(side, low, ((1,), (1,)))


def own_kernel(nfreq, nclass, kappa, coeff, green, facing, other, swept, operator, inverse, first, second):
    part = lax.div(lax.axis_index("par"), nfreq)
    cells = green.shape[1]
    blocks = cells // LANES
    parts = coeff.shape[0] // blocks
    extent = cells + 2 * REACH

    def inv(index):
        return 1.0 / (4.0 + chosen(kappa, index, nclass, lambda t, k: t[k]))

    def column(value):
        return jnp.transpose(jnp.broadcast_to(value, (LANES, LANES)))

    before = inv(coeff[pl.ds(jnp.maximum(part * blocks - 1, 0), 1), :])
    after = inv(coeff[pl.ds(jnp.minimum((part + 1) * blocks, parts * blocks - 1), 1), :])
    inside = inv(coeff[pl.ds(pl.multiple_of(part * blocks, blocks), blocks), :])
    inverse[0:REACH] = column(jnp.where(part > 0, before, 0.0))[LANES - REACH :]
    inverse[extent - REACH : extent] = column(jnp.where(part < parts - 1, after, 0.0))[:REACH]
    for b in range(blocks):
        inverse[REACH + b * LANES : REACH + (b + 1) * LANES] = column(inside[b : b + 1])

    odd = lax.rem(part, 2) == 1
    near, far = planes(facing.at[1], 0, REACH), planes(other, 0, REACH)
    operator[0:REACH] = jnp.where(odd, near, far)
    operator[REACH : REACH + cells] = planes(green, 0, cells)
    operator[extent - REACH : extent] = jnp.where(odd, far, near)

    hood = stencil()
    none = jnp.zeros((DIP, 2 * LANES), BF16)
    for ref in (first, second):
        ref[0:DIP] = none
        ref[DIP + extent : 2 * DIP + extent] = none

    def solved(at, value):
        scale = inverse[at : at + LANES]
        return jnp.concatenate([scale, scale], axis=1) * value

    for at in range(0, extent, LANES):
        value = solved(at, operator[at : at + LANES].astype(F32))
        first[DIP + at : DIP + at + LANES] = value.astype(BF16)
    for at in range(0, extent, LANES):
        total = operator[at : at + LANES].astype(F32) + dot(hood, first[at : at + LANES + 2 * DIP])
        second[DIP + at : DIP + at + LANES] = solved(at, total).astype(BF16)
    for at in range(REACH, REACH + cells, LANES):
        total = operator[at : at + LANES].astype(F32) + dot(hood, second[at : at + LANES + 2 * DIP])
        swept[:, at - REACH : at - REACH + LANES] = jnp.transpose(solved(at, total)).astype(BF16)


def cross_kernel(swept, *refs):
    greens, pairs = refs[: len(refs) // 2], refs[len(refs) // 2 :]
    for green, pair in zip(greens, pairs):
        pair[0], pair[1] = halves(dot(swept[...], planes(green, 0, green.shape[1])))


def data_of(nsens, weight, refs):
    terms = [applied(v[...], p[0], p[1]) for v, p in zip(refs[:nsens], refs[nsens:])]
    return weight[...] * sum(terms[1:], terms[0])


def keep_kernel(nsens, weight, *refs):
    data = data_of(nsens, weight, refs[:-1])
    half = data.shape[0] // 2
    for k in range(2):
        refs[-1][k] = data[k * half : (k + 1) * half]


def send_kernel(nfreq, nsens, weight, *refs):
    refs, (*sends, total) = refs[: 2 * nsens], refs[2 * nsens :]
    par = lax.axis_index("par")
    part, odd = lax.div(par, nfreq), lax.rem(par, 2)
    total[...] = data_of(nsens, weight, refs)
    half = total.shape[0] // 2
    rows = half // (SPLIT - 1)
    for send, step in zip(sends, ROUTES):
        place = 0
        for core, route in enumerate(step):
            for p, q in enumerate(route):
                place = jnp.where((part == p) & (odd == core), PLACE[p ^ max(q, 0)], place)
        for k in range(2):
            send[k] = total[pl.ds(pl.multiple_of(k * half + place * rows, rows), rows), :].astype(BF16)


def shards(probes, green_blocks, noise_table, station_class, kappa_table, coeff_index):
    nfreq = noise_table.shape[0]
    nsens = lax.axis_size("sens")
    sensors, rows_dev = probes.shape[1:]
    cells = green_blocks.shape[1]
    smem = pl.BlockSpec(memory_space=pltpu.SMEM)
    vmem = pl.BlockSpec(memory_space=pltpu.VMEM)
    greens = [turned(green_blocks, "sens", k) for k in range(1, nsens)]
    vector = jnp.transpose(probes, (0, 2, 1))
    partner = swapped(vector, "par", 2 * nfreq)

    rim = jax.ShapeDtypeStruct((2, REACH, sensors), BF16)
    weight, held, facing, other = pl.pallas_call(
        functools.partial(prep_kernel, nfreq),
        out_shape=[
            jax.ShapeDtypeStruct((1, sensors), F32),
            jax.ShapeDtypeStruct((2, rows_dev, sensors), BF16),
            rim,
            rim,
        ],
        in_specs=[smem] + [vmem] * 3,
        out_specs=[vmem] * 4,
        compiler_params=PARAMS,
        cost_estimate=PRIOR,
        name="prep",
    )(noise_table, station_class.reshape(1, -1), vector, green_blocks)

    mine = jnp.stack([held, partner])
    sent = jnp.stack([mine.reshape(2, -1, sensors), facing])
    got = swapped(sent, "par", nfreq)
    other = crossed(other, "par", nfreq)
    vectors = jnp.concatenate([mine, got[0].reshape(mine.shape)], axis=0)
    vectors = (weight * vectors.astype(F32)).astype(BF16)
    kept, given = vectors[:1], vectors[1:]
    given, kept = lax.optimization_barrier((given, kept))
    rests = [[turned(v, "sens", k) for k in range(1, nsens)] for v in (given, kept)]
    rows = SPLIT * rows_dev
    extent = cells + 2 * REACH
    swept = pl.pallas_call(
        functools.partial(own_kernel, nfreq, kappa_table.shape[0]),
        out_shape=jax.ShapeDtypeStruct((2 * sensors, cells), BF16),
        in_specs=[smem] + [vmem] * 4,
        out_specs=vmem,
        scratch_shapes=[
            pltpu.VMEM((extent, 2 * sensors), BF16),
            pltpu.VMEM((extent, LANES), F32),
            pltpu.VMEM((extent + 2 * DIP, 2 * sensors), BF16),
            pltpu.VMEM((extent + 2 * DIP, 2 * sensors), BF16),
        ],
        compiler_params=PARAMS,
        cost_estimate=BESIDE,
        name="own",
    )(kappa_table, coeff_index.reshape(-1, LANES), green_blocks, got, other)
    pairs = pl.pallas_call(
        cross_kernel,
        out_shape=[jax.ShapeDtypeStruct((2, sensors, 2 * sensors), BF16)] * nsens,
        in_specs=[vmem] * (1 + nsens),
        out_specs=[vmem] * nsens,
        compiler_params=PARAMS,
        cost_estimate=PRIOR,
        name="cross",
    )(swept, green_blocks, *greens)
    sends = list(pl.pallas_call(
        functools.partial(send_kernel, nfreq, nsens),
        out_shape=[jax.ShapeDtypeStruct((2, rows_dev, sensors), BF16)] * len(ROUTES),
        in_specs=[vmem] * (1 + 2 * nsens),
        out_specs=[vmem] * len(ROUTES),
        scratch_shapes=[pltpu.VMEM((2 * (rows - rows_dev), sensors), F32)],
        compiler_params=PARAMS,
        name="send",
    )(weight, given, *rests[0], *pairs))
    sends[2], rests[1] = lax.optimization_barrier((sends[2], rests[1]))
    shares = [routed(send, "par", nfreq, step) for send, step in zip(sends, ROUTES)]
    shares[0], kept = lax.optimization_barrier((shares[0], kept))
    keep = pl.pallas_call(
        functools.partial(keep_kernel, nsens),
        out_shape=jax.ShapeDtypeStruct((2, rows_dev, sensors), F32),
        in_specs=[vmem] * (1 + 2 * nsens),
        out_specs=vmem,
        compiler_params=PARAMS,
        cost_estimate=PRIOR,
        name="keep",
    )(weight, kept, *rests[1], *pairs)
    par = lax.axis_index("par")
    for step, share in zip(ROUTES, shares):
        share = share.astype(F32)
        keep = lax.optimization_barrier(keep)
        for core, route in enumerate(step):
            for q in range(SPLIT):
                if q not in route:
                    share = jnp.where((par // nfreq == q) & (par % 2 == core), 0.0, share)
        keep = keep + share
    return jnp.transpose(keep, (0, 2, 1))


def solution(mesh):
    in_specs = (P(None, "sens", "par"), P(None, "par", "sens"), P(), P("sens"), P(), P())
    out_specs = P(None, "sens", "par")
    return jax.shard_map(shards, mesh=mesh, in_specs=in_specs, out_specs=out_specs, check_vma=False)
```

```python
import functools

import jax
import jax.numpy as jnp
from jax import lax
from jax.experimental import pallas as pl
from jax.experimental.pallas import tpu as pltpu
from jax.sharding import PartitionSpec as P

SPLIT = 4
DIP = 32
LANES = 128
ROUTES = (((1, 2, 3, 0), (3, 2, 1, 0)), ((-1, -1, 0, -1), (2, -1, -1, -1)), ((3, 0, 1, 2), (1, 3, 0, 2)), ((2, 3, -1, 1), (-1, 0, 3, 1)))
PLACE = (0, 1, 0, 2)
REACH = 2 * DIP
F32 = jnp.float32
BF16 = jnp.bfloat16
PRIOR = pl.CostEstimate(flops=1, bytes_accessed=1, transcendentals=0)
BESIDE = pl.CostEstimate(flops=575_000_000, bytes_accessed=1, transcendentals=0)
PARAMS = pltpu.CompilerParams(vmem_limit_bytes=32 * 2**20)


def swapped(value, axis, mask):
    return lax.ppermute(value, axis, [(i, i ^ mask) for i in range(lax.axis_size(axis))])


def turned(value, axis, step):
    size = lax.axis_size(axis)
    return lax.ppermute(value, axis, [(i, (i + step) % size) for i in range(size)])


def crossed(value, axis, nfreq):
    pairs = []
    for i in range(lax.axis_size(axis)):
        part = i // nfreq
        outer = part in (0, SPLIT - 1)
        pairs.append((i, i ^ 1 if outer else i + nfreq if part % 2 else i - nfreq))
    return lax.ppermute(value, axis, pairs)


def routed(value, axis, nfreq, step):
    pairs = []
    for i in range(lax.axis_size(axis)):
        part, to = i // nfreq, step[i % 2][i // nfreq]
        pairs.append((i, i ^ 1 if to < 0 else i + (to - part) * nfreq))
    return lax.ppermute(value, axis, pairs)


def dot(a, b, form=((1,), (0,))):
    return lax.dot_general(a, b, (form, ((), ())), preferred_element_type=F32)


def chosen(table, index):
    value = jnp.zeros(index.shape, F32)
    for k in range(table.shape[1]):
        value = jnp.where(index == k, jnp.broadcast_to(table[:, k : k + 1], index.shape), value)
    return value


def stencil():
    row = lax.broadcasted_iota(jnp.int32, (LANES, LANES + 2 * DIP), 0)
    col = lax.broadcasted_iota(jnp.int32, (LANES, LANES + 2 * DIP), 1)
    away = col - DIP - row
    dip = lax.rem(row, DIP)
    hit = (away == DIP) | (away == -DIP)
    hit = hit | ((away == 1) & (dip != DIP - 1)) | ((away == -1) & (dip != 0))
    return hit.astype(F32).astype(BF16)


def planes(ref, b, n):
    return jnp.concatenate([ref[0, b : b + n], ref[1, b : b + n]], axis=1)


def lhs(z):
    rows = z.shape[0] * z.shape[2]
    zr, zi = z[:, 0].reshape(rows, LANES), z[:, 1].reshape(rows, LANES)
    top = jnp.concatenate([zr, zi], axis=1)
    return jnp.concatenate([top, jnp.concatenate([zi, -zr], axis=1)], axis=0)


def prep_kernel(nfreq, noise, station, vector, green, weight, held, facing, other):
    par = lax.axis_index("par")
    freq, part = lax.rem(par, nfreq), lax.div(par, nfreq)
    odd = lax.rem(part, 2)
    cells = green.shape[1]
    first = pl.multiple_of(odd * (cells - REACH), REACH)
    last = pl.multiple_of((1 - odd) * (cells - REACH), REACH)
    held[...] = vector[...]
    facing[...] = green[:, pl.ds(last, REACH)]
    other[...] = green[:, pl.ds(first, REACH)]
    variance = chosen(noise[pl.ds(freq, 1), :], station[...])
    weight[...] = 1.0 / jnp.sqrt(variance)


def halves(full):
    real = full[:LANES, :LANES] + full[LANES:, LANES:]
    imag = full[:LANES, LANES:] - full[LANES:, :LANES]
    return jnp.concatenate([real, imag], axis=1).astype(BF16)


def applied(z, product):
    return dot(lhs(z), product, ((1,), (1,)))


def own_kernel(nfreq, kappa, coeff, green, facing, other, swept, operator, inverse, first, second):
    part = lax.div(lax.axis_index("par"), nfreq)
    cells = green.shape[1]
    blocks = cells // LANES
    parts = coeff.shape[0] // blocks
    extent = cells + 2 * REACH

    def inv(index):
        return 1.0 / (4.0 + chosen(kappa[...], index))

    def column(value):
        return jnp.transpose(jnp.broadcast_to(value, (LANES, LANES)))

    before = inv(coeff[pl.ds(jnp.maximum(part * blocks - 1, 0), 1), :])
    after = inv(coeff[pl.ds(jnp.minimum((part + 1) * blocks, parts * blocks - 1), 1), :])
    inside = inv(coeff[pl.ds(pl.multiple_of(part * blocks, blocks), blocks), :])
    inverse[0:REACH] = column(jnp.where(part > 0, before, 0.0))[LANES - REACH :]
    inverse[extent - REACH : extent] = column(jnp.where(part < parts - 1, after, 0.0))[:REACH]
    for b in range(blocks):
        inverse[REACH + b * LANES : REACH + (b + 1) * LANES] = column(inside[b : b + 1])

    odd = lax.rem(part, 2) == 1
    near, far = planes(facing.at[1], 0, REACH), planes(other, 0, REACH)
    operator[0:REACH] = jnp.where(odd, near, far)
    operator[REACH : REACH + cells] = planes(green, 0, cells)
    operator[extent - REACH : extent] = jnp.where(odd, far, near)

    hood = stencil()
    none = jnp.zeros((DIP, 2 * LANES), BF16)
    for ref in (first, second):
        ref[0:DIP] = none
        ref[DIP + extent : 2 * DIP + extent] = none

    def solved(at, value):
        scale = inverse[at : at + LANES]
        return jnp.concatenate([scale, scale], axis=1) * value

    for at in range(0, extent, LANES):
        value = solved(at, operator[at : at + LANES].astype(F32))
        first[DIP + at : DIP + at + LANES] = value.astype(BF16)
    for at in range(0, extent, LANES):
        total = operator[at : at + LANES].astype(F32) + dot(hood, first[at : at + LANES + 2 * DIP])
        second[DIP + at : DIP + at + LANES] = solved(at, total).astype(BF16)
    for at in range(REACH, REACH + cells, LANES):
        total = operator[at : at + LANES].astype(F32) + dot(hood, second[at : at + LANES + 2 * DIP])
        swept[:, at - REACH : at - REACH + LANES] = jnp.transpose(solved(at, total)).astype(BF16)


def cross_kernel(swept, *refs):
    greens, pairs = refs[: len(refs) // 2], refs[len(refs) // 2 :]
    for green, pair in zip(greens, pairs):
        pair[...] = halves(dot(swept[...], planes(green, 0, green.shape[1])))


def data_of(nsens, weight, refs):
    terms = [applied(v[...], p[...]) for v, p in zip(refs[:nsens], refs[nsens:])]
    return weight[...] * sum(terms[1:], terms[0])


def keep_kernel(nsens, weight, *refs):
    data = data_of(nsens, weight, refs[:-1])
    half = data.shape[0] // 2
    for k in range(2):
        refs[-1][k] = data[k * half : (k + 1) * half]


def send_kernel(nfreq, nsens, weight, *refs):
    refs, (*sends, total) = refs[: 2 * nsens], refs[2 * nsens :]
    par = lax.axis_index("par")
    part, odd = lax.div(par, nfreq), lax.rem(par, 2)
    total[...] = data_of(nsens, weight, refs)
    half = total.shape[0] // 2
    rows = half // (SPLIT - 1)
    for send, step in zip(sends, ROUTES):
        place = 0
        for core, route in enumerate(step):
            for p, q in enumerate(route):
                place = jnp.where((part == p) & (odd == core), PLACE[p ^ max(q, 0)], place)
        for k in range(2):
            send[k] = total[pl.ds(pl.multiple_of(k * half + place * rows, rows), rows), :].astype(BF16)


def shards(probes, green_blocks, noise_table, station_class, kappa_table, coeff_index):
    nfreq = noise_table.shape[0]
    nsens = lax.axis_size("sens")
    sensors, rows_dev = probes.shape[1:]
    cells = green_blocks.shape[1]
    vmem = pl.BlockSpec(memory_space=pltpu.VMEM)
    greens = [turned(green_blocks, "sens", k) for k in range(1, nsens)]
    vector = jnp.transpose(probes, (0, 2, 1))
    partner = swapped(vector, "par", 2 * nfreq)

    rim = jax.ShapeDtypeStruct((2, REACH, sensors), BF16)
    weight, held, facing, other = pl.pallas_call(
        functools.partial(prep_kernel, nfreq),
        out_shape=[
            jax.ShapeDtypeStruct((1, sensors), F32),
            jax.ShapeDtypeStruct((2, rows_dev, sensors), BF16),
            rim,
            rim,
        ],
        in_specs=[vmem] * 4,
        out_specs=[vmem] * 4,
        compiler_params=PARAMS,
        cost_estimate=PRIOR,
        name="prep",
    )(noise_table, station_class.reshape(1, -1), vector, green_blocks)

    mine = jnp.stack([held, partner])
    sent = jnp.stack([mine.reshape(2, -1, sensors), facing])
    got = swapped(sent, "par", nfreq)
    other = crossed(other, "par", nfreq)
    vectors = jnp.concatenate([mine, got[0].reshape(mine.shape)], axis=0)
    vectors = (weight * vectors.astype(F32)).astype(BF16)
    kept, given = vectors[:1], vectors[1:]
    given, kept = lax.optimization_barrier((given, kept))
    rests = [[turned(v, "sens", k) for k in range(1, nsens)] for v in (given, kept)]
    rows = SPLIT * rows_dev
    extent = cells + 2 * REACH
    swept = pl.pallas_call(
        functools.partial(own_kernel, nfreq),
        out_shape=jax.ShapeDtypeStruct((2 * sensors, cells), BF16),
        in_specs=[vmem] * 5,
        out_specs=vmem,
        scratch_shapes=[
            pltpu.VMEM((extent, 2 * sensors), BF16),
            pltpu.VMEM((extent, LANES), F32),
            pltpu.VMEM((extent + 2 * DIP, 2 * sensors), BF16),
            pltpu.VMEM((extent + 2 * DIP, 2 * sensors), BF16),
        ],
        compiler_params=PARAMS,
        cost_estimate=BESIDE,
        name="own",
    )(kappa_table.reshape(1, -1), coeff_index.reshape(-1, LANES), green_blocks, got, other)
    pairs = pl.pallas_call(
        cross_kernel,
        out_shape=[jax.ShapeDtypeStruct((sensors, 2 * sensors), BF16)] * nsens,
        in_specs=[vmem] * (1 + nsens),
        out_specs=[vmem] * nsens,
        compiler_params=PARAMS,
        cost_estimate=PRIOR,
        name="cross",
    )(swept, green_blocks, *greens)
    sends = list(pl.pallas_call(
        functools.partial(send_kernel, nfreq, nsens),
        out_shape=[jax.ShapeDtypeStruct((2, rows_dev, sensors), BF16)] * len(ROUTES),
        in_specs=[vmem] * (1 + 2 * nsens),
        out_specs=[vmem] * len(ROUTES),
        scratch_shapes=[pltpu.VMEM((2 * (rows - rows_dev), sensors), F32)],
        compiler_params=PARAMS,
        name="send",
    )(weight, given, *rests[0], *pairs))
    sends[2], rests[1] = lax.optimization_barrier((sends[2], rests[1]))
    shares = [routed(send, "par", nfreq, step) for send, step in zip(sends, ROUTES)]
    shares[0], kept = lax.optimization_barrier((shares[0], kept))
    keep = pl.pallas_call(
        functools.partial(keep_kernel, nsens),
        out_shape=jax.ShapeDtypeStruct((2, rows_dev, sensors), F32),
        in_specs=[vmem] * (1 + 2 * nsens),
        out_specs=vmem,
        compiler_params=PARAMS,
        cost_estimate=PRIOR,
        name="keep",
    )(weight, kept, *rests[1], *pairs)
    par = lax.axis_index("par")
    for step, share in zip(ROUTES, shares):
        share = share.astype(F32)
        keep = lax.optimization_barrier(keep)
        for core, route in enumerate(step):
            for q in range(SPLIT):
                if q not in route:
                    share = jnp.where((par // nfreq == q) & (par % 2 == core), 0.0, share)
        keep = keep + share
    return jnp.transpose(keep, (0, 2, 1))


def solution(mesh):
    in_specs = (P(None, "sens", "par"), P(None, "par", "sens"), P(), P("sens"), P(), P())
    out_specs = P(None, "sens", "par")
    return jax.shard_map(shards, mesh=mesh, in_specs=in_specs, out_specs=out_specs, check_vma=False)
```

```python
import functools

import jax
import jax.numpy as jnp
from jax import lax
from jax.experimental import pallas as pl
from jax.experimental.pallas import tpu as pltpu
from jax.sharding import PartitionSpec as P

SPLIT = 4
DIP = 32
LANES = 128
ROUTES = (((1, 2, 3, 0), (3, 2, 1, 0)), ((-1, -1, 0, -1), (2, -1, -1, -1)), ((3, 0, 1, 2), (1, 3, 0, 2)), ((2, 3, -1, 1), (-1, 0, 3, 1)))
PLACE = (0, 1, 0, 2)
REACH = 2 * DIP
F32 = jnp.float32
BF16 = jnp.bfloat16
PRIOR = pl.CostEstimate(flops=1, bytes_accessed=1, transcendentals=0)
BESIDE = pl.CostEstimate(flops=575_000_000, bytes_accessed=1, transcendentals=0)
PARAMS = pltpu.CompilerParams(vmem_limit_bytes=32 * 2**20)


def swapped(value, axis, mask):
    return lax.ppermute(value, axis, [(i, i ^ mask) for i in range(lax.axis_size(axis))])


def turned(value, axis, step):
    size = lax.axis_size(axis)
    return lax.ppermute(value, axis, [(i, (i + step) % size) for i in range(size)])


def crossed(value, axis, nfreq):
    pairs = []
    for i in range(lax.axis_size(axis)):
        part = i // nfreq
        outer = part in (0, SPLIT - 1)
        pairs.append((i, i ^ 1 if outer else i + nfreq if part % 2 else i - nfreq))
    return lax.ppermute(value, axis, pairs)


def routed(value, axis, nfreq, step):
    pairs = []
    for i in range(lax.axis_size(axis)):
        part, to = i // nfreq, step[i % 2][i // nfreq]
        pairs.append((i, i ^ 1 if to < 0 else i + (to - part) * nfreq))
    return lax.ppermute(value, axis, pairs)


def dot(a, b, form=((1,), (0,))):
    return lax.dot_general(a, b, (form, ((), ())), preferred_element_type=F32)


def chosen(table, index):
    value = jnp.zeros(index.shape, F32)
    for k in range(table.shape[1]):
        value = jnp.where(index == k, jnp.broadcast_to(table[:, k : k + 1], index.shape), value)
    return value


def stencil():
    row = lax.broadcasted_iota(jnp.int32, (LANES, LANES + 2 * DIP), 0)
    col = lax.broadcasted_iota(jnp.int32, (LANES, LANES + 2 * DIP), 1)
    away = col - DIP - row
    dip = lax.rem(row, DIP)
    hit = (away == DIP) | (away == -DIP)
    hit = hit | ((away == 1) & (dip != DIP - 1)) | ((away == -1) & (dip != 0))
    return hit.astype(F32).astype(BF16)


def planes(ref, b, n):
    return jnp.concatenate([ref[0, b : b + n], ref[1, b : b + n]], axis=1)


def lhs(z):
    rows = z.shape[0] * z.shape[2]
    zr, zi = z[:, 0].reshape(rows, LANES), z[:, 1].reshape(rows, LANES)
    top = jnp.concatenate([zr, zi], axis=1)
    return jnp.concatenate([top, jnp.concatenate([zi, -zr], axis=1)], axis=0)


def prep_kernel(nfreq, noise, station, vector, green, weight, held, facing, other):
    par = lax.axis_index("par")
    freq, part = lax.rem(par, nfreq), lax.div(par, nfreq)
    odd = lax.rem(part, 2)
    cells = green.shape[1]
    first = pl.multiple_of(odd * (cells - REACH), REACH)
    last = pl.multiple_of((1 - odd) * (cells - REACH), REACH)
    held[...] = vector[...]
    facing[...] = green[:, pl.ds(last, REACH)]
    other[...] = green[:, pl.ds(first, REACH)]
    variance = chosen(noise[pl.ds(freq, 1), :], station[...])
    weight[...] = 1.0 / jnp.sqrt(variance)


def halves(full):
    real = full[:LANES, :LANES] + full[LANES:, LANES:]
    imag = full[:LANES, LANES:] - full[LANES:, :LANES]
    return jnp.concatenate([real, imag], axis=1).astype(BF16)


def applied(z, product):
    return dot(lhs(z), product, ((1,), (1,)))


def own_kernel(nfreq, weight, kappa, coeff, green, facing, other, swept, operator, inverse, first, second):
    part = lax.div(lax.axis_index("par"), nfreq)
    cells = green.shape[1]
    blocks = cells // LANES
    parts = coeff.shape[0] // blocks
    extent = cells + 2 * REACH

    def inv(index):
        return 1.0 / (4.0 + chosen(kappa[...], index))

    def column(value):
        return jnp.transpose(jnp.broadcast_to(value, (LANES, LANES)))

    before = inv(coeff[pl.ds(jnp.maximum(part * blocks - 1, 0), 1), :])
    after = inv(coeff[pl.ds(jnp.minimum((part + 1) * blocks, parts * blocks - 1), 1), :])
    inside = inv(coeff[pl.ds(pl.multiple_of(part * blocks, blocks), blocks), :])
    inverse[0:REACH] = column(jnp.where(part > 0, before, 0.0))[LANES - REACH :]
    inverse[extent - REACH : extent] = column(jnp.where(part < parts - 1, after, 0.0))[:REACH]
    for b in range(blocks):
        inverse[REACH + b * LANES : REACH + (b + 1) * LANES] = column(inside[b : b + 1])

    odd = lax.rem(part, 2) == 1
    near, far = planes(facing.at[1], 0, REACH), planes(other, 0, REACH)
    operator[0:REACH] = jnp.where(odd, near, far)
    operator[REACH : REACH + cells] = planes(green, 0, cells)
    operator[extent - REACH : extent] = jnp.where(odd, far, near)

    wide = jnp.concatenate([weight[...]] * 2, axis=1)
    hood = stencil()
    none = jnp.zeros((DIP, 2 * LANES), BF16)
    for ref in (first, second):
        ref[0:DIP] = none
        ref[DIP + extent : 2 * DIP + extent] = none

    def solved(at, value):
        scale = inverse[at : at + LANES]
        return jnp.concatenate([scale, scale], axis=1) * value

    for at in range(0, extent, LANES):
        value = solved(at, operator[at : at + LANES].astype(F32))
        first[DIP + at : DIP + at + LANES] = value.astype(BF16)
    for at in range(0, extent, LANES):
        total = operator[at : at + LANES].astype(F32) + dot(hood, first[at : at + LANES + 2 * DIP])
        second[DIP + at : DIP + at + LANES] = solved(at, total).astype(BF16)
    for at in range(REACH, REACH + cells, LANES):
        total = operator[at : at + LANES].astype(F32) + dot(hood, second[at : at + LANES + 2 * DIP])
        swept[:, at - REACH : at - REACH + LANES] = jnp.transpose(wide * solved(at, total)).astype(BF16)


def cross_kernel(swept, *refs):
    greens, pairs = refs[: len(refs) // 2], refs[len(refs) // 2 :]
    for green, pair in zip(greens, pairs):
        pair[...] = halves(dot(swept[...], planes(green, 0, green.shape[1])))


def data_of(nsens, refs):
    terms = [applied(v[...], p[...]) for v, p in zip(refs[:nsens], refs[nsens:])]
    return sum(terms[1:], terms[0])


def keep_kernel(nsens, *refs):
    data = data_of(nsens, refs[:-1])
    half = data.shape[0] // 2
    for k in range(2):
        refs[-1][k] = data[k * half : (k + 1) * half]


def send_kernel(nfreq, nsens, *refs):
    refs, sends = refs[: 2 * nsens], refs[2 * nsens :]
    par = lax.axis_index("par")
    part, odd = lax.div(par, nfreq), lax.rem(par, 2)
    data = data_of(nsens, refs)
    half = data.shape[0] // 2
    rows = half // (SPLIT - 1)
    for send, step in zip(sends, ROUTES):
        place = 0
        for core, route in enumerate(step):
            for p, q in enumerate(route):
                place = jnp.where((part == p) & (odd == core), PLACE[p ^ max(q, 0)], place)
        for k in range(2):
            blocks = [data[k * half + j * rows : k * half + (j + 1) * rows] for j in range(SPLIT - 1)]
            share = blocks[0]
            for j, block in enumerate(blocks[1:], 1):
                share = jnp.where(place == j, block, share)
            send[k] = share.astype(BF16)


def shards(probes, green_blocks, noise_table, station_class, kappa_table, coeff_index):
    nfreq = noise_table.shape[0]
    nsens = lax.axis_size("sens")
    sensors, rows_dev = probes.shape[1:]
    cells = green_blocks.shape[1]
    vmem = pl.BlockSpec(memory_space=pltpu.VMEM)
    greens = [turned(green_blocks, "sens", k) for k in range(1, nsens)]
    vector = jnp.transpose(probes, (0, 2, 1))
    partner = swapped(vector, "par", 2 * nfreq)

    rim = jax.ShapeDtypeStruct((2, REACH, sensors), BF16)
    weight, held, facing, other = pl.pallas_call(
        functools.partial(prep_kernel, nfreq),
        out_shape=[
            jax.ShapeDtypeStruct((1, sensors), F32),
            jax.ShapeDtypeStruct((2, rows_dev, sensors), BF16),
            rim,
            rim,
        ],
        in_specs=[vmem] * 4,
        out_specs=[vmem] * 4,
        compiler_params=PARAMS,
        cost_estimate=PRIOR,
        name="prep",
    )(noise_table, station_class.reshape(1, -1), vector, green_blocks)

    mine = jnp.stack([held, partner])
    sent = jnp.stack([mine.reshape(2, -1, sensors), facing])
    got = swapped(sent, "par", nfreq)
    other = crossed(other, "par", nfreq)
    vectors = jnp.concatenate([mine, got[0].reshape(mine.shape)], axis=0)
    vectors = (weight * vectors.astype(F32)).astype(BF16)
    kept, given = vectors[:1], vectors[1:]
    given, kept = lax.optimization_barrier((given, kept))
    rests = [[turned(v, "sens", k) for k in range(1, nsens)] for v in (given, kept)]
    rows = SPLIT * rows_dev
    extent = cells + 2 * REACH
    swept = pl.pallas_call(
        functools.partial(own_kernel, nfreq),
        out_shape=jax.ShapeDtypeStruct((2 * sensors, cells), BF16),
        in_specs=[vmem] * 6,
        out_specs=vmem,
        scratch_shapes=[
            pltpu.VMEM((extent, 2 * sensors), BF16),
            pltpu.VMEM((extent, LANES), F32),
            pltpu.VMEM((extent + 2 * DIP, 2 * sensors), BF16),
            pltpu.VMEM((extent + 2 * DIP, 2 * sensors), BF16),
        ],
        compiler_params=PARAMS,
        cost_estimate=BESIDE,
        name="own",
    )(weight, kappa_table.reshape(1, -1), coeff_index.reshape(-1, LANES), green_blocks, got, other)
    pairs = pl.pallas_call(
        cross_kernel,
        out_shape=[jax.ShapeDtypeStruct((sensors, 2 * sensors), BF16)] * nsens,
        in_specs=[vmem] * (1 + nsens),
        out_specs=[vmem] * nsens,
        compiler_params=PARAMS,
        cost_estimate=PRIOR,
        name="cross",
    )(swept, green_blocks, *greens)
    sends = list(pl.pallas_call(
        functools.partial(send_kernel, nfreq, nsens),
        out_shape=[jax.ShapeDtypeStruct((2, rows_dev, sensors), BF16)] * len(ROUTES),
        in_specs=[vmem] * (2 * nsens),
        out_specs=[vmem] * len(ROUTES),
        compiler_params=PARAMS,
        name="send",
    )(given, *rests[0], *pairs))
    sends[2], rests[1] = lax.optimization_barrier((sends[2], rests[1]))
    shares = [routed(send, "par", nfreq, step) for send, step in zip(sends, ROUTES)]
    shares[0], kept = lax.optimization_barrier((shares[0], kept))
    keep = pl.pallas_call(
        functools.partial(keep_kernel, nsens),
        out_shape=jax.ShapeDtypeStruct((2, rows_dev, sensors), F32),
        in_specs=[vmem] * (2 * nsens),
        out_specs=vmem,
        compiler_params=PARAMS,
        cost_estimate=PRIOR,
        name="keep",
    )(kept, *rests[1], *pairs)
    par = lax.axis_index("par")
    for step, share in zip(ROUTES, shares):
        share = share.astype(F32)
        keep = lax.optimization_barrier(keep)
        for core, route in enumerate(step):
            for q in range(SPLIT):
                if q not in route:
                    share = jnp.where((par // nfreq == q) & (par % 2 == core), 0.0, share)
        keep = keep + share
    return jnp.transpose(keep, (0, 2, 1))


def solution(mesh):
    in_specs = (P(None, "sens", "par"), P(None, "par", "sens"), P(), P("sens"), P(), P())
    out_specs = P(None, "sens", "par")
    return jax.shard_map(shards, mesh=mesh, in_specs=in_specs, out_specs=out_specs, check_vma=False)
```

```python
import functools

import jax
import jax.numpy as jnp
from jax import lax
from jax.experimental import pallas as pl
from jax.experimental.pallas import tpu as pltpu
from jax.sharding import PartitionSpec as P

SPLIT = 4
DIP = 32
LANES = 128
ROUTES = (((-1, -1, 0, -1), (2, -1, -1, -1)), ((1, 2, 3, 0), (1, 3, 0, 2)), ((3, 0, 1, 2), (3, 2, 1, 0)), ((2, 3, -1, 1), (-1, 0, 3, 1)))
PLACE = (0, 1, 0, 2)
REACH = 2 * DIP
F32 = jnp.float32
BF16 = jnp.bfloat16
PRIOR = pl.CostEstimate(flops=1, bytes_accessed=1, transcendentals=0)
BESIDE = pl.CostEstimate(flops=575_000_000, bytes_accessed=1, transcendentals=0)
PARAMS = pltpu.CompilerParams(vmem_limit_bytes=32 * 2**20)


def swapped(value, axis, mask):
    return lax.ppermute(value, axis, [(i, i ^ mask) for i in range(lax.axis_size(axis))])


def turned(value, axis, step):
    size = lax.axis_size(axis)
    return lax.ppermute(value, axis, [(i, (i + step) % size) for i in range(size)])


def crossed(value, axis, nfreq):
    pairs = []
    for i in range(lax.axis_size(axis)):
        part = i // nfreq
        outer = part in (0, SPLIT - 1)
        pairs.append((i, i ^ 1 if outer else i + nfreq if part % 2 else i - nfreq))
    return lax.ppermute(value, axis, pairs)


def routed(value, axis, nfreq, step):
    pairs = []
    for i in range(lax.axis_size(axis)):
        part, to = i // nfreq, step[i % 2][i // nfreq]
        pairs.append((i, i ^ 1 if to < 0 else i + (to - part) * nfreq))
    return lax.ppermute(value, axis, pairs)


def dot(a, b, form=((1,), (0,))):
    return lax.dot_general(a, b, (form, ((), ())), preferred_element_type=F32)


def chosen(table, index):
    value = jnp.zeros(index.shape, F32)
    for k in range(table.shape[1]):
        value = jnp.where(index == k, jnp.broadcast_to(table[:, k : k + 1], index.shape), value)
    return value


def stencil():
    row = lax.broadcasted_iota(jnp.int32, (LANES, LANES + 2 * DIP), 0)
    col = lax.broadcasted_iota(jnp.int32, (LANES, LANES + 2 * DIP), 1)
    away = col - DIP - row
    dip = lax.rem(row, DIP)
    hit = (away == DIP) | (away == -DIP)
    hit = hit | ((away == 1) & (dip != DIP - 1)) | ((away == -1) & (dip != 0))
    return hit.astype(F32).astype(BF16)


def planes(ref, b, n):
    return jnp.concatenate([ref[0, b : b + n], ref[1, b : b + n]], axis=1)


def lhs(z):
    rows = z.shape[0] * z.shape[2]
    zr, zi = z[:, 0].reshape(rows, LANES), z[:, 1].reshape(rows, LANES)
    top = jnp.concatenate([zr, zi], axis=1)
    return jnp.concatenate([top, jnp.concatenate([zi, -zr], axis=1)], axis=0)


def prep_kernel(nfreq, noise, station, vector, green, weight, held, facing, other):
    par = lax.axis_index("par")
    freq, part = lax.rem(par, nfreq), lax.div(par, nfreq)
    odd = lax.rem(part, 2)
    cells = green.shape[1]
    first = pl.multiple_of(odd * (cells - REACH), REACH)
    last = pl.multiple_of((1 - odd) * (cells - REACH), REACH)
    held[...] = vector[...]
    facing[...] = green[:, pl.ds(last, REACH)]
    other[...] = green[:, pl.ds(first, REACH)]
    variance = chosen(noise[pl.ds(freq, 1), :], station[...])
    weight[...] = 1.0 / jnp.sqrt(variance)


def halves(full):
    real = full[:LANES, :LANES] + full[LANES:, LANES:]
    imag = full[:LANES, LANES:] - full[LANES:, :LANES]
    return jnp.concatenate([real, imag], axis=1).astype(BF16)


def applied(z, product):
    return dot(lhs(z), product, ((1,), (1,)))


def own_kernel(nfreq, weight, kappa, coeff, green, facing, other, swept, operator, inverse, first, second):
    part = lax.div(lax.axis_index("par"), nfreq)
    cells = green.shape[1]
    blocks = cells // LANES
    parts = coeff.shape[0] // blocks
    extent = cells + 2 * REACH

    def inv(index):
        return 1.0 / (4.0 + chosen(kappa[...], index))

    def column(value):
        return jnp.transpose(jnp.broadcast_to(value, (LANES, LANES)))

    before = inv(coeff[pl.ds(jnp.maximum(part * blocks - 1, 0), 1), :])
    after = inv(coeff[pl.ds(jnp.minimum((part + 1) * blocks, parts * blocks - 1), 1), :])
    inside = inv(coeff[pl.ds(pl.multiple_of(part * blocks, blocks), blocks), :])
    inverse[0:REACH] = column(jnp.where(part > 0, before, 0.0))[LANES - REACH :]
    inverse[extent - REACH : extent] = column(jnp.where(part < parts - 1, after, 0.0))[:REACH]
    for b in range(blocks):
        inverse[REACH + b * LANES : REACH + (b + 1) * LANES] = column(inside[b : b + 1])

    odd = lax.rem(part, 2) == 1
    near, far = planes(facing.at[1], 0, REACH), planes(other, 0, REACH)
    operator[0:REACH] = jnp.where(odd, near, far)
    operator[REACH : REACH + cells] = planes(green, 0, cells)
    operator[extent - REACH : extent] = jnp.where(odd, far, near)

    wide = jnp.concatenate([weight[...]] * 2, axis=1)
    hood = stencil()
    none = jnp.zeros((DIP, 2 * LANES), BF16)
    for ref in (first, second):
        ref[0:DIP] = none
        ref[DIP + extent : 2 * DIP + extent] = none

    def solved(at, value):
        scale = inverse[at : at + LANES]
        return jnp.concatenate([scale, scale], axis=1) * value

    for at in range(0, extent, LANES):
        value = solved(at, operator[at : at + LANES].astype(F32))
        first[DIP + at : DIP + at + LANES] = value.astype(BF16)
    for at in range(0, extent, LANES):
        total = operator[at : at + LANES].astype(F32) + dot(hood, first[at : at + LANES + 2 * DIP])
        second[DIP + at : DIP + at + LANES] = solved(at, total).astype(BF16)
    for at in range(REACH, REACH + cells, LANES):
        total = operator[at : at + LANES].astype(F32) + dot(hood, second[at : at + LANES + 2 * DIP])
        swept[:, at - REACH : at - REACH + LANES] = jnp.transpose(wide * solved(at, total)).astype(BF16)


def cross_kernel(swept, *refs):
    greens, pairs = refs[: len(refs) // 2], refs[len(refs) // 2 :]
    for green, pair in zip(greens, pairs):
        pair[...] = halves(dot(swept[...], planes(green, 0, green.shape[1])))


def data_of(nsens, refs):
    terms = [applied(v[...], p[...]) for v, p in zip(refs[:nsens], refs[nsens:])]
    return sum(terms[1:], terms[0])


def keep_kernel(nsens, *refs):
    data = data_of(nsens, refs[:-1])
    half = data.shape[0] // 2
    for k in range(2):
        refs[-1][k] = data[k * half : (k + 1) * half]


def send_kernel(nfreq, nsens, *refs):
    refs, sends = refs[: 2 * nsens], refs[2 * nsens :]
    par = lax.axis_index("par")
    part, odd = lax.div(par, nfreq), lax.rem(par, 2)
    data = data_of(nsens, refs)
    half = data.shape[0] // 2
    rows = half // (SPLIT - 1)
    for send, step in zip(sends, ROUTES):
        place = 0
        for core, route in enumerate(step):
            for p, q in enumerate(route):
                place = jnp.where((part == p) & (odd == core), PLACE[p ^ max(q, 0)], place)
        for k in range(2):
            blocks = [data[k * half + j * rows : k * half + (j + 1) * rows] for j in range(SPLIT - 1)]
            share = blocks[0]
            for j, block in enumerate(blocks[1:], 1):
                share = jnp.where(place == j, block, share)
            send[k] = share.astype(BF16)


def shards(probes, green_blocks, noise_table, station_class, kappa_table, coeff_index):
    nfreq = noise_table.shape[0]
    nsens = lax.axis_size("sens")
    sensors, rows_dev = probes.shape[1:]
    cells = green_blocks.shape[1]
    vmem = pl.BlockSpec(memory_space=pltpu.VMEM)
    greens = [turned(green_blocks, "sens", k) for k in range(1, nsens)]
    vector = jnp.transpose(probes, (0, 2, 1))
    partner = swapped(vector, "par", 2 * nfreq)

    rim = jax.ShapeDtypeStruct((2, REACH, sensors), BF16)
    weight, held, facing, other = pl.pallas_call(
        functools.partial(prep_kernel, nfreq),
        out_shape=[
            jax.ShapeDtypeStruct((1, sensors), F32),
            jax.ShapeDtypeStruct((2, rows_dev, sensors), BF16),
            rim,
            rim,
        ],
        in_specs=[vmem] * 4,
        out_specs=[vmem] * 4,
        compiler_params=PARAMS,
        cost_estimate=PRIOR,
        name="prep",
    )(noise_table, station_class.reshape(1, -1), vector, green_blocks)

    mine = jnp.stack([held, partner])
    sent = jnp.stack([mine.reshape(2, -1, sensors), facing])
    got = swapped(sent, "par", nfreq)
    other = crossed(other, "par", nfreq)
    vectors = jnp.concatenate([mine, got[0].reshape(mine.shape)], axis=0)
    vectors = (weight * vectors.astype(F32)).astype(BF16)
    kept, given = vectors[:1], vectors[1:]
    given, kept = lax.optimization_barrier((given, kept))
    rests = [[turned(v, "sens", k) for k in range(1, nsens)] for v in (given, kept)]
    rows = SPLIT * rows_dev
    extent = cells + 2 * REACH
    swept = pl.pallas_call(
        functools.partial(own_kernel, nfreq),
        out_shape=jax.ShapeDtypeStruct((2 * sensors, cells), BF16),
        in_specs=[vmem] * 6,
        out_specs=vmem,
        scratch_shapes=[
            pltpu.VMEM((extent, 2 * sensors), BF16),
            pltpu.VMEM((extent, LANES), F32),
            pltpu.VMEM((extent + 2 * DIP, 2 * sensors), BF16),
            pltpu.VMEM((extent + 2 * DIP, 2 * sensors), BF16),
        ],
        compiler_params=PARAMS,
        cost_estimate=BESIDE,
        name="own",
    )(weight, kappa_table.reshape(1, -1), coeff_index.reshape(-1, LANES), green_blocks, got, other)
    pairs = pl.pallas_call(
        cross_kernel,
        out_shape=[jax.ShapeDtypeStruct((sensors, 2 * sensors), BF16)] * nsens,
        in_specs=[vmem] * (1 + nsens),
        out_specs=[vmem] * nsens,
        compiler_params=PARAMS,
        cost_estimate=PRIOR,
        name="cross",
    )(swept, green_blocks, *greens)
    sends = list(pl.pallas_call(
        functools.partial(send_kernel, nfreq, nsens),
        out_shape=[jax.ShapeDtypeStruct((2, rows_dev, sensors), BF16)] * len(ROUTES),
        in_specs=[vmem] * (2 * nsens),
        out_specs=[vmem] * len(ROUTES),
        compiler_params=PARAMS,
        name="send",
    )(given, *rests[0], *pairs))
    sends[2], rests[1] = lax.optimization_barrier((sends[2], rests[1]))
    shares = [routed(send, "par", nfreq, step) for send, step in zip(sends, ROUTES)]
    shares[0], kept = lax.optimization_barrier((shares[0], kept))
    keep = pl.pallas_call(
        functools.partial(keep_kernel, nsens),
        out_shape=jax.ShapeDtypeStruct((2, rows_dev, sensors), F32),
        in_specs=[vmem] * (2 * nsens),
        out_specs=vmem,
        compiler_params=PARAMS,
        cost_estimate=PRIOR,
        name="keep",
    )(kept, *rests[1], *pairs)
    par = lax.axis_index("par")
    for step, share in zip(ROUTES, shares):
        share = share.astype(F32)
        keep = lax.optimization_barrier(keep)
        for core, route in enumerate(step):
            for q in range(SPLIT):
                if q not in route:
                    share = jnp.where((par // nfreq == q) & (par % 2 == core), 0.0, share)
        keep = keep + share
    return jnp.transpose(keep, (0, 2, 1))


def solution(mesh):
    in_specs = (P(None, "sens", "par"), P(None, "par", "sens"), P(), P("sens"), P(), P())
    out_specs = P(None, "sens", "par")
    return jax.shard_map(shards, mesh=mesh, in_specs=in_specs, out_specs=out_specs, check_vma=False)
```

```python
import functools

import jax
import jax.numpy as jnp
from jax import lax
from jax.experimental import pallas as pl
from jax.experimental.pallas import tpu as pltpu
from jax.sharding import PartitionSpec as P

SPLIT = 4
DIP = 32
LANES = 128
ROUTES = (((-1, -1, 0, -1), (2, -1, -1, -1)), ((1, 2, 3, 0), (1, 3, 0, 2)), ((3, 0, 1, 2), (3, 2, 1, 0)), ((2, 3, -1, 1), (-1, 0, 3, 1)))
PLACE = (0, 1, 0, 2)
REACH = 2 * DIP
F32 = jnp.float32
BF16 = jnp.bfloat16
PRIOR = pl.CostEstimate(flops=1, bytes_accessed=1, transcendentals=0)
BESIDE = pl.CostEstimate(flops=575_000_000, bytes_accessed=1, transcendentals=0)
PARAMS = pltpu.CompilerParams(vmem_limit_bytes=32 * 2**20)


def swapped(value, axis, mask):
    return lax.ppermute(value, axis, [(i, i ^ mask) for i in range(lax.axis_size(axis))])


def turned(value, axis, step):
    size = lax.axis_size(axis)
    return lax.ppermute(value, axis, [(i, (i + step) % size) for i in range(size)])


def crossed(value, axis, nfreq):
    pairs = []
    for i in range(lax.axis_size(axis)):
        part = i // nfreq
        outer = part in (0, SPLIT - 1)
        pairs.append((i, i ^ 1 if outer else i + nfreq if part % 2 else i - nfreq))
    return lax.ppermute(value, axis, pairs)


def routed(value, axis, nfreq, step):
    pairs = []
    for i in range(lax.axis_size(axis)):
        part, to = i // nfreq, step[i % 2][i // nfreq]
        pairs.append((i, i ^ 1 if to < 0 else i + (to - part) * nfreq))
    return lax.ppermute(value, axis, pairs)


def dot(a, b, form=((1,), (0,))):
    return lax.dot_general(a, b, (form, ((), ())), preferred_element_type=F32)


def chosen(table, index):
    value = jnp.zeros(index.shape, F32)
    for k in range(table.shape[1]):
        value = jnp.where(index == k, jnp.broadcast_to(table[:, k : k + 1], index.shape), value)
    return value


def stencil():
    row = lax.broadcasted_iota(jnp.int32, (LANES, LANES + 2 * DIP), 0)
    col = lax.broadcasted_iota(jnp.int32, (LANES, LANES + 2 * DIP), 1)
    away = col - DIP - row
    dip = lax.rem(row, DIP)
    hit = (away == DIP) | (away == -DIP)
    hit = hit | ((away == 1) & (dip != DIP - 1)) | ((away == -1) & (dip != 0))
    return hit.astype(F32).astype(BF16)


def planes(ref, b, n):
    return jnp.concatenate([ref[0, b : b + n], ref[1, b : b + n]], axis=1)


def lhs(z):
    rows = z.shape[0] * z.shape[2]
    zr, zi = z[:, 0].reshape(rows, LANES), z[:, 1].reshape(rows, LANES)
    top = jnp.concatenate([zr, zi], axis=1)
    return jnp.concatenate([top, jnp.concatenate([zi, -zr], axis=1)], axis=0)


def prep_kernel(nfreq, noise, station, vector, green, weight, held, facing, other):
    par = lax.axis_index("par")
    freq, part = lax.rem(par, nfreq), lax.div(par, nfreq)
    odd = lax.rem(part, 2)
    cells = green.shape[1]
    first = pl.multiple_of(odd * (cells - REACH), REACH)
    last = pl.multiple_of((1 - odd) * (cells - REACH), REACH)
    held[...] = vector[...]
    facing[...] = green[:, pl.ds(last, REACH)]
    other[...] = green[:, pl.ds(first, REACH)]
    variance = chosen(noise[pl.ds(freq, 1), :], station[...])
    weight[...] = 1.0 / jnp.sqrt(variance)


def halves(full):
    real = full[:LANES, :LANES] + full[LANES:, LANES:]
    imag = full[:LANES, LANES:] - full[LANES:, :LANES]
    return jnp.concatenate([real, imag], axis=1).astype(BF16)


def applied(z, product):
    return dot(lhs(z), product, ((1,), (1,)))


def own_kernel(nfreq, weight, kappa, coeff, green, facing, other, swept, operator, inverse, first, second):
    part = lax.div(lax.axis_index("par"), nfreq)
    cells = green.shape[1]
    blocks = cells // LANES
    parts = coeff.shape[0] // blocks
    extent = cells + 2 * REACH

    def inv(index):
        return 1.0 / (4.0 + chosen(kappa[...], index))

    def column(value):
        return jnp.transpose(jnp.broadcast_to(value, (LANES, LANES)))

    before = inv(coeff[pl.ds(jnp.maximum(part * blocks - 1, 0), 1), :])
    after = inv(coeff[pl.ds(jnp.minimum((part + 1) * blocks, parts * blocks - 1), 1), :])
    inside = inv(coeff[pl.ds(pl.multiple_of(part * blocks, blocks), blocks), :])
    inverse[0:REACH] = column(jnp.where(part > 0, before, 0.0))[LANES - REACH :]
    inverse[extent - REACH : extent] = column(jnp.where(part < parts - 1, after, 0.0))[:REACH]
    for b in range(blocks):
        inverse[REACH + b * LANES : REACH + (b + 1) * LANES] = column(inside[b : b + 1])

    odd = lax.rem(part, 2) == 1
    near, far = planes(facing.at[1], 0, REACH), planes(other, 0, REACH)
    operator[0:REACH] = jnp.where(odd, near, far)
    operator[REACH : REACH + cells] = planes(green, 0, cells)
    operator[extent - REACH : extent] = jnp.where(odd, far, near)

    wide = jnp.concatenate([weight[...]] * 2, axis=1)
    hood = stencil()
    none = jnp.zeros((DIP, 2 * LANES), BF16)
    for ref in (first, second):
        ref[0:DIP] = none
        ref[DIP + extent : 2 * DIP + extent] = none

    def solved(at, value):
        scale = inverse[at : at + LANES]
        return jnp.concatenate([scale, scale], axis=1) * value

    for at in range(0, extent, LANES):
        value = solved(at, operator[at : at + LANES].astype(F32))
        first[DIP + at : DIP + at + LANES] = value.astype(BF16)
    for at in range(0, extent, LANES):
        total = operator[at : at + LANES].astype(F32) + dot(hood, first[at : at + LANES + 2 * DIP])
        second[DIP + at : DIP + at + LANES] = solved(at, total).astype(BF16)
    for at in range(REACH, REACH + cells, LANES):
        total = operator[at : at + LANES].astype(F32) + dot(hood, second[at : at + LANES + 2 * DIP])
        swept[:, at - REACH : at - REACH + LANES] = jnp.transpose(wide * solved(at, total)).astype(BF16)


def cross_kernel(swept, *refs):
    greens, pairs = refs[: len(refs) // 2], refs[len(refs) // 2 :]
    for green, pair in zip(greens, pairs):
        pair[...] = halves(dot(swept[...], planes(green, 0, green.shape[1])))


def data_of(nsens, refs):
    terms = [applied(v[...], p[...]) for v, p in zip(refs[:nsens], refs[nsens:])]
    return sum(terms[1:], terms[0])


def keep_kernel(nsens, *refs):
    data = data_of(nsens, refs[:-1])
    half = data.shape[0] // 2
    for k in range(2):
        refs[-1][k] = data[k * half : (k + 1) * half]


def send_kernel(nfreq, nsens, *refs):
    refs, sends = refs[: 2 * nsens], refs[2 * nsens :]
    par = lax.axis_index("par")
    part, odd = lax.div(par, nfreq), lax.rem(par, 2)
    data = data_of(nsens, refs)
    half = data.shape[0] // 2
    rows = half // (SPLIT - 1)
    for send, step in zip(sends, ROUTES):
        place = 0
        for core, route in enumerate(step):
            for p, q in enumerate(route):
                place = jnp.where((part == p) & (odd == core), PLACE[p ^ max(q, 0)], place)
        for k in range(2):
            blocks = [data[k * half + j * rows : k * half + (j + 1) * rows] for j in range(SPLIT - 1)]
            share = blocks[0]
            for j, block in enumerate(blocks[1:], 1):
                share = jnp.where(place == j, block, share)
            send[k] = share.astype(BF16)


def shards(probes, green_blocks, noise_table, station_class, kappa_table, coeff_index):
    nfreq = noise_table.shape[0]
    nsens = lax.axis_size("sens")
    sensors, rows_dev = probes.shape[1:]
    cells = green_blocks.shape[1]
    vmem = pl.BlockSpec(memory_space=pltpu.VMEM)
    greens = [turned(green_blocks, "sens", k) for k in range(1, nsens)]
    vector = jnp.transpose(probes, (0, 2, 1))
    partner = swapped(vector, "par", 2 * nfreq)

    rim = jax.ShapeDtypeStruct((2, REACH, sensors), BF16)
    weight, held, facing, other = pl.pallas_call(
        functools.partial(prep_kernel, nfreq),
        out_shape=[
            jax.ShapeDtypeStruct((1, sensors), F32),
            jax.ShapeDtypeStruct((2, rows_dev, sensors), BF16),
            rim,
            rim,
        ],
        in_specs=[vmem] * 4,
        out_specs=[vmem] * 4,
        compiler_params=PARAMS,
        cost_estimate=PRIOR,
        name="prep",
    )(noise_table, station_class.reshape(1, -1), vector, green_blocks)

    mine = jnp.stack([held, partner])
    sent = jnp.stack([mine.reshape(2, -1, sensors), facing])
    got = swapped(sent, "par", nfreq)
    other = crossed(other, "par", nfreq)
    vectors = jnp.concatenate([mine, got[0].reshape(mine.shape)], axis=0)
    vectors = (weight * vectors.astype(F32)).astype(BF16)
    kept, given = vectors[:1], vectors[1:]
    given, kept = lax.optimization_barrier((given, kept))
    rests = [[turned(v, "sens", k) for k in range(1, nsens)] for v in (given, kept)]
    rows = SPLIT * rows_dev
    extent = cells + 2 * REACH
    swept = pl.pallas_call(
        functools.partial(own_kernel, nfreq),
        out_shape=jax.ShapeDtypeStruct((2 * sensors, cells), BF16),
        in_specs=[vmem] * 6,
        out_specs=vmem,
        scratch_shapes=[
            pltpu.VMEM((extent, 2 * sensors), BF16),
            pltpu.VMEM((extent, LANES), F32),
            pltpu.VMEM((extent + 2 * DIP, 2 * sensors), BF16),
            pltpu.VMEM((extent + 2 * DIP, 2 * sensors), BF16),
        ],
        compiler_params=PARAMS,
        cost_estimate=BESIDE,
        name="own",
    )(weight, kappa_table.reshape(1, -1), coeff_index.reshape(-1, LANES), green_blocks, got, other)
    pairs = pl.pallas_call(
        cross_kernel,
        out_shape=[jax.ShapeDtypeStruct((sensors, 2 * sensors), BF16)] * nsens,
        in_specs=[vmem] * (1 + nsens),
        out_specs=[vmem] * nsens,
        compiler_params=PARAMS,
        cost_estimate=PRIOR,
        name="cross",
    )(swept, green_blocks, *greens)
    sends = list(pl.pallas_call(
        functools.partial(send_kernel, nfreq, nsens),
        out_shape=[jax.ShapeDtypeStruct((2, rows_dev, sensors), BF16)] * len(ROUTES),
        in_specs=[vmem] * (2 * nsens),
        out_specs=[vmem] * len(ROUTES),
        compiler_params=PARAMS,
        name="send",
    )(given, *rests[0], *pairs))
    sends[1], rests[1] = lax.optimization_barrier((sends[1], rests[1]))
    shares = [routed(send, "par", nfreq, step) for send, step in zip(sends, ROUTES)]
    shares[0], kept = lax.optimization_barrier((shares[0], kept))
    keep = pl.pallas_call(
        functools.partial(keep_kernel, nsens),
        out_shape=jax.ShapeDtypeStruct((2, rows_dev, sensors), F32),
        in_specs=[vmem] * (2 * nsens),
        out_specs=vmem,
        compiler_params=PARAMS,
        cost_estimate=PRIOR,
        name="keep",
    )(kept, *rests[1], *pairs)
    par = lax.axis_index("par")
    for step, share in zip(ROUTES, shares):
        share = share.astype(F32)
        keep = lax.optimization_barrier(keep)
        for core, route in enumerate(step):
            for q in range(SPLIT):
                if q not in route:
                    share = jnp.where((par // nfreq == q) & (par % 2 == core), 0.0, share)
        keep = keep + share
    return jnp.transpose(keep, (0, 2, 1))


def solution(mesh):
    in_specs = (P(None, "sens", "par"), P(None, "par", "sens"), P(), P("sens"), P(), P())
    out_specs = P(None, "sens", "par")
    return jax.shard_map(shards, mesh=mesh, in_specs=in_specs, out_specs=out_specs, check_vma=False)
```

```python
import functools

import jax
import jax.numpy as jnp
from jax import lax
from jax.experimental import pallas as pl
from jax.experimental.pallas import tpu as pltpu
from jax.sharding import PartitionSpec as P

SPLIT = 4
DIP = 32
LANES = 128
ROUTES = (((-1, -1, 0, -1), (2, -1, -1, -1)), ((1, 2, 3, 0), (1, 3, 0, 2)), ((3, 0, 1, 2), (3, 2, 1, 0)), ((2, 3, -1, 1), (-1, 0, 3, 1)))
PLACE = (0, 1, 0, 2)
REACH = 2 * DIP
F32 = jnp.float32
BF16 = jnp.bfloat16
PRIOR = pl.CostEstimate(flops=1, bytes_accessed=1, transcendentals=0)
BESIDE = pl.CostEstimate(flops=575_000_000, bytes_accessed=1, transcendentals=0)
PARAMS = pltpu.CompilerParams(vmem_limit_bytes=32 * 2**20)


def swapped(value, axis, mask):
    return lax.ppermute(value, axis, [(i, i ^ mask) for i in range(lax.axis_size(axis))])


def turned(value, axis, step):
    size = lax.axis_size(axis)
    return lax.ppermute(value, axis, [(i, (i + step) % size) for i in range(size)])


def crossed(value, axis, nfreq):
    pairs = []
    for i in range(lax.axis_size(axis)):
        part = i // nfreq
        outer = part in (0, SPLIT - 1)
        pairs.append((i, i ^ 1 if outer else i + nfreq if part % 2 else i - nfreq))
    return lax.ppermute(value, axis, pairs)


def routed(value, axis, nfreq, step):
    pairs = []
    for i in range(lax.axis_size(axis)):
        part, to = i // nfreq, step[i % 2][i // nfreq]
        pairs.append((i, i ^ 1 if to < 0 else i + (to - part) * nfreq))
    return lax.ppermute(value, axis, pairs)


def dot(a, b, form=((1,), (0,))):
    return lax.dot_general(a, b, (form, ((), ())), preferred_element_type=F32)


def chosen(table, index):
    value = jnp.zeros(index.shape, F32)
    for k in range(table.shape[1]):
        value = jnp.where(index == k, jnp.broadcast_to(table[:, k : k + 1], index.shape), value)
    return value


def stencil():
    row = lax.broadcasted_iota(jnp.int32, (LANES, LANES + 2 * DIP), 0)
    col = lax.broadcasted_iota(jnp.int32, (LANES, LANES + 2 * DIP), 1)
    away = col - DIP - row
    dip = lax.rem(row, DIP)
    hit = (away == DIP) | (away == -DIP)
    hit = hit | ((away == 1) & (dip != DIP - 1)) | ((away == -1) & (dip != 0))
    return hit.astype(F32).astype(BF16)


def planes(ref, b, n):
    return jnp.concatenate([ref[0, b : b + n], ref[1, b : b + n]], axis=1)


def lhs(z):
    rows = z.shape[0] * z.shape[2]
    zr, zi = z[:, 0].reshape(rows, LANES), z[:, 1].reshape(rows, LANES)
    top = jnp.concatenate([zr, zi], axis=1)
    return jnp.concatenate([top, jnp.concatenate([zi, -zr], axis=1)], axis=0)


def prep_kernel(nfreq, noise, station, vector, green, weight, held, facing, other):
    par = lax.axis_index("par")
    freq, part = lax.rem(par, nfreq), lax.div(par, nfreq)
    odd = lax.rem(part, 2)
    cells = green.shape[1]
    first = pl.multiple_of(odd * (cells - REACH), REACH)
    last = pl.multiple_of((1 - odd) * (cells - REACH), REACH)
    held[...] = vector[...]
    facing[...] = green[:, pl.ds(last, REACH)]
    other[...] = green[:, pl.ds(first, REACH)]
    variance = chosen(noise[pl.ds(freq, 1), :], station[...])
    weight[...] = 1.0 / jnp.sqrt(variance)


def halves(full):
    real = full[:LANES, :LANES] + full[LANES:, LANES:]
    imag = full[:LANES, LANES:] - full[LANES:, :LANES]
    return jnp.concatenate([real, imag], axis=1).astype(BF16)


def applied(z, product):
    return dot(lhs(z), product, ((1,), (1,)))


def own_kernel(nfreq, weight, kappa, coeff, green, facing, other, swept, operator, inverse, first, second):
    part = lax.div(lax.axis_index("par"), nfreq)
    cells = green.shape[1]
    blocks = cells // LANES
    parts = coeff.shape[0] // blocks
    extent = cells + 2 * REACH

    def inv(index):
        return 1.0 / (4.0 + chosen(kappa[...], index))

    def column(value):
        return jnp.transpose(jnp.broadcast_to(value, (LANES, LANES)))

    before = inv(coeff[pl.ds(jnp.maximum(part * blocks - 1, 0), 1), :])
    after = inv(coeff[pl.ds(jnp.minimum((part + 1) * blocks, parts * blocks - 1), 1), :])
    inside = inv(coeff[pl.ds(pl.multiple_of(part * blocks, blocks), blocks), :])
    inverse[0:REACH] = column(jnp.where(part > 0, before, 0.0))[LANES - REACH :]
    inverse[extent - REACH : extent] = column(jnp.where(part < parts - 1, after, 0.0))[:REACH]
    for b in range(blocks):
        inverse[REACH + b * LANES : REACH + (b + 1) * LANES] = column(inside[b : b + 1])

    odd = lax.rem(part, 2) == 1
    near, far = planes(facing.at[1], 0, REACH), planes(other, 0, REACH)
    operator[0:REACH] = jnp.where(odd, near, far)
    operator[REACH : REACH + cells] = planes(green, 0, cells)
    operator[extent - REACH : extent] = jnp.where(odd, far, near)

    wide = jnp.concatenate([weight[...]] * 2, axis=1)
    hood = stencil()
    none = jnp.zeros((DIP, 2 * LANES), BF16)
    for ref in (first, second):
        ref[0:DIP] = none
        ref[DIP + extent : 2 * DIP + extent] = none

    def solved(at, value):
        scale = inverse[at : at + LANES]
        return jnp.concatenate([scale, scale], axis=1) * value

    for at in range(0, extent, LANES):
        value = solved(at, operator[at : at + LANES].astype(F32))
        first[DIP + at : DIP + at + LANES] = value.astype(BF16)
    for at in range(0, extent, LANES):
        total = operator[at : at + LANES].astype(F32) + dot(hood, first[at : at + LANES + 2 * DIP])
        second[DIP + at : DIP + at + LANES] = solved(at, total).astype(BF16)
    for at in range(REACH, REACH + cells, LANES):
        total = operator[at : at + LANES].astype(F32) + dot(hood, second[at : at + LANES + 2 * DIP])
        swept[:, at - REACH : at - REACH + LANES] = jnp.transpose(wide * solved(at, total)).astype(BF16)


def cross_kernel(swept, *refs):
    greens, pairs = refs[: len(refs) // 2], refs[len(refs) // 2 :]
    for green, pair in zip(greens, pairs):
        pair[...] = halves(dot(swept[...], planes(green, 0, green.shape[1])))


def data_of(nsens, refs):
    terms = [applied(v[...], p[...]) for v, p in zip(refs[:nsens], refs[nsens:])]
    return sum(terms[1:], terms[0])


def keep_kernel(nsens, *refs):
    data = data_of(nsens, refs[:-1])
    half = data.shape[0] // 2
    for k in range(2):
        refs[-1][k] = data[k * half : (k + 1) * half]


def send_kernel(nfreq, nsens, *refs):
    refs, sends = refs[: 2 * nsens], refs[2 * nsens :]
    par = lax.axis_index("par")
    part, odd = lax.div(par, nfreq), lax.rem(par, 2)
    data = data_of(nsens, refs)
    half = data.shape[0] // 2
    rows = half // (SPLIT - 1)
    for send, step in zip(sends, ROUTES):
        place = 0
        for core, route in enumerate(step):
            for p, q in enumerate(route):
                place = jnp.where((part == p) & (odd == core), PLACE[p ^ max(q, 0)], place)
        for k in range(2):
            blocks = [data[k * half + j * rows : k * half + (j + 1) * rows] for j in range(SPLIT - 1)]
            share = blocks[0]
            for j, block in enumerate(blocks[1:], 1):
                share = jnp.where(place == j, block, share)
            send[k] = share.astype(BF16)


def shards(probes, green_blocks, noise_table, station_class, kappa_table, coeff_index):
    nfreq = noise_table.shape[0]
    nsens = lax.axis_size("sens")
    sensors, rows_dev = probes.shape[1:]
    cells = green_blocks.shape[1]
    vmem = pl.BlockSpec(memory_space=pltpu.VMEM)
    greens = [turned(green_blocks, "sens", k) for k in range(1, nsens)]
    vector = jnp.transpose(probes, (0, 2, 1))
    partner = swapped(vector, "par", 2 * nfreq)

    rim = jax.ShapeDtypeStruct((2, REACH, sensors), BF16)
    weight, held, facing, other = pl.pallas_call(
        functools.partial(prep_kernel, nfreq),
        out_shape=[
            jax.ShapeDtypeStruct((1, sensors), F32),
            jax.ShapeDtypeStruct((2, rows_dev, sensors), BF16),
            rim,
            rim,
        ],
        in_specs=[vmem] * 4,
        out_specs=[vmem] * 4,
        compiler_params=PARAMS,
        cost_estimate=PRIOR,
        name="prep",
    )(noise_table, station_class.reshape(1, -1), vector, green_blocks)

    mine = jnp.stack([held, partner])
    sent = jnp.stack([mine.reshape(2, -1, sensors), facing])
    got = swapped(sent, "par", nfreq)
    other = crossed(other, "par", nfreq)
    vectors = jnp.concatenate([mine, got[0].reshape(mine.shape)], axis=0)
    vectors = (weight * vectors.astype(F32)).astype(BF16)
    kept, given = vectors[:1], vectors[1:]
    given, kept = lax.optimization_barrier((given, kept))
    rests = [[turned(v, "sens", k) for k in range(1, nsens)] for v in (given, kept)]
    rows = SPLIT * rows_dev
    extent = cells + 2 * REACH
    swept = pl.pallas_call(
        functools.partial(own_kernel, nfreq),
        out_shape=jax.ShapeDtypeStruct((2 * sensors, cells), BF16),
        in_specs=[vmem] * 6,
        out_specs=vmem,
        scratch_shapes=[
            pltpu.VMEM((extent, 2 * sensors), BF16),
            pltpu.VMEM((extent, LANES), F32),
            pltpu.VMEM((extent + 2 * DIP, 2 * sensors), BF16),
            pltpu.VMEM((extent + 2 * DIP, 2 * sensors), BF16),
        ],
        compiler_params=PARAMS,
        cost_estimate=BESIDE,
        name="own",
    )(weight, kappa_table.reshape(1, -1), coeff_index.reshape(-1, LANES), green_blocks, got, other)
    pairs = pl.pallas_call(
        cross_kernel,
        out_shape=[jax.ShapeDtypeStruct((sensors, 2 * sensors), BF16)] * nsens,
        in_specs=[vmem] * (1 + nsens),
        out_specs=[vmem] * nsens,
        compiler_params=PARAMS,
        cost_estimate=PRIOR,
        name="cross",
    )(swept, green_blocks, *greens)
    sends = list(pl.pallas_call(
        functools.partial(send_kernel, nfreq, nsens),
        out_shape=[jax.ShapeDtypeStruct((2, rows_dev, sensors), BF16)] * len(ROUTES),
        in_specs=[vmem] * (2 * nsens),
        out_specs=[vmem] * len(ROUTES),
        compiler_params=PARAMS,
        name="send",
    )(given, *rests[0], *pairs))
    sends[3], rests[1] = lax.optimization_barrier((sends[3], rests[1]))
    shares = [routed(send, "par", nfreq, step) for send, step in zip(sends, ROUTES)]
    shares[0], kept = lax.optimization_barrier((shares[0], kept))
    keep = pl.pallas_call(
        functools.partial(keep_kernel, nsens),
        out_shape=jax.ShapeDtypeStruct((2, rows_dev, sensors), F32),
        in_specs=[vmem] * (2 * nsens),
        out_specs=vmem,
        compiler_params=PARAMS,
        cost_estimate=PRIOR,
        name="keep",
    )(kept, *rests[1], *pairs)
    par = lax.axis_index("par")
    for step, share in zip(ROUTES, shares):
        share = share.astype(F32)
        keep = lax.optimization_barrier(keep)
        for core, route in enumerate(step):
            for q in range(SPLIT):
                if q not in route:
                    share = jnp.where((par // nfreq == q) & (par % 2 == core), 0.0, share)
        keep = keep + share
    return jnp.transpose(keep, (0, 2, 1))


def solution(mesh):
    in_specs = (P(None, "sens", "par"), P(None, "par", "sens"), P(), P("sens"), P(), P())
    out_specs = P(None, "sens", "par")
    return jax.shard_map(shards, mesh=mesh, in_specs=in_specs, out_specs=out_specs, check_vma=False)
```
